128 devices in a mesh: inter: 16 (over z_lo, y, core), intra: 8 (over x, z_hi).
Axes of the slice: x: 4, y: 4, z: 4 (z_hi: 2, z_lo: 2; z = z_hi * 2 + z_lo), core: 2. Of those that a mesh axis runs over, the one named last changes fastest.
Arguments:
- layer_input: bfloat16 [24576, 3584], P(('inter', 'intra')), may hold values from -6 to 6
- up_cotangent: bfloat16 [24576, 10240], P(('inter', 'intra')), may hold values from -24 to 24
- master: float32 [10240, 3584], P(('intra', 'inter')), may hold values from -0.6 to 0.6
- first_moment: float32 [10240, 3584], P(('intra', 'inter')), may hold values from -6 to 6
- second_moment: float32 [10240, 3584], P(('intra', 'inter')), may hold values from 0.2 to 0.5
Outputs:
- new_master: float32 [10240, 3584], P(('intra', 'inter'))
- new_first: float32 [10240, 3584], P(('intra', 'inter'))
- new_second: float32 [10240, 3584], P(('intra', 'inter'))
- new_copy: bfloat16 [10240, 3584], P('intra')
The draws below stay inside these ranges and needn't reach their ends.
All inputs are finite; a program needn't handle non-finite values.
Results may differ from the reference program's by a relative error of at most 0.015.
Values may be sent and summed in bfloat16 or wider, within the bound.
No kernel may reach another device: no remote copies, remote signals or barrier semaphores. Data moves between devices by JAX's collectives and lax.ppermute only.
A program may use at most 128 MiB of HBM per device.

```python
import math
import jax
import jax.numpy as jnp
from jax import lax

COLS = 3584
BUCKET = 10240
TOKENS = 24576


def spiked(values, own_key, source, target, shards_of, factor):
    def block_of(position):
        return (jnp.arange(values.shape[position]) // (values.shape[position] // shards_of)).reshape((-1,) + (1,) * (values.ndim - 1 - position))

    near = jax.random.permutation(own_key, shards_of)[block_of(target)]
    other_side = (block_of(target) + shards_of // 2) % shards_of
    return jnp.where((block_of(source) == near) | (block_of(source) == other_side), factor * values, values)


def level_of(key, dims, shards, smallest, largest):
    factor_of, own = 1.0, jax.random.fold_in(key, 6)
    for dim, shards_of in shards:
        heights = jnp.exp(jax.random.uniform(jax.random.fold_in(own, dim), (shards_of,), jnp.float32, smallest / len(shards), largest / len(shards)))
        factor_of = factor_of * jnp.repeat(heights, dims[dim] // shards_of).reshape([-1 if axis == dim else 1 for axis in range(len(dims))])
    return factor_of


def centred(stream_key, shape, deviation, bound, shards=(), kind=jnp.bfloat16):
    array = deviation * jax.random.normal(stream_key, shape, jnp.float32)
    if shards:
        array = array * level_of(stream_key, shape, shards, -0.22, 0.18)
    return jnp.clip(array, -bound, bound).astype(kind)


def gaussian_with(stream_key, shape, scale, reach, split, heavy, held_as=jnp.bfloat16):
    result = scale * jax.random.normal(stream_key, shape, jnp.float32)
    if split:
        result = result * level_of(stream_key, shape, split, -0.22, 0.18)
    return jnp.clip(spiked(result, jax.random.fold_in(stream_key, 3), *heavy), -reach, reach).astype(held_as)


def setup_inputs(seed: int = 0) -> dict:
    key_list = jax.random.split(jax.random.key(seed), 6)
    return {
        "layer_input": centred(key_list[0], (TOKENS, COLS), 1.0, 6.0, ((0, 128),)),
        "up_cotangent": gaussian_with(key_list[1], (TOKENS, BUCKET), 1.0, 24.0, ((0, 128),), (0, 1, 128, 5.5)),
        "master": centred(key_list[2], (BUCKET, COLS), 0.1, 0.6, ((0, 128),), jnp.float32),
        "first_moment": centred(key_list[3], (BUCKET, COLS), 1.0, 6.0, ((0, 128),), jnp.float32),
        "second_moment": jnp.clip(jnp.exp(math.log(0.5) - 0.9162907 * jax.random.uniform(key_list[4], (BUCKET, COLS), jnp.float32) ** level_of(key_list[4], (BUCKET, COLS), ((0, 128),), -0.2, 0.2)), 0.2, 0.5),
    }


def adamw(grad, master, first_moment, second_moment):
    new_first = 0.9 * first_moment + 0.1 * grad
    new_second = 0.95 * second_moment + 0.05 * (grad * grad)
    first_hat = new_first / (1.0 - 0.9 ** 10)
    second_hat = new_second / (1.0 - 0.95 ** 10)
    step_dir = first_hat / (jnp.sqrt(second_hat) + 1e-08) + 0.1 * master
    new_master = master - 0.02 * step_dir
    return (new_master, new_first, new_second)

def reference(layer_input, up_cotangent, master, first_moment, second_moment):
    summed = lax.dot_general(up_cotangent, layer_input, (((0,), (0,)), ((), ())), preferred_element_type=jnp.float32)
    grad = summed * (1.0 / math.sqrt(TOKENS))
    new_master, new_first, new_second = adamw(grad, master, first_moment, second_moment)
    new_copy = new_master.astype(jnp.bfloat16)
    return (new_master, new_first, new_second, new_copy)
```

```python
import functools
import math

import jax
import jax.numpy as jnp
from jax import lax
from jax.experimental import pallas as pl
from jax.experimental.pallas import tpu as pltpu
from jax.sharding import PartitionSpec as P

AXES = ("inter", "intra")
WIDTHS = (1024, 768)


def device(x, y, z, c):
    inter = (z % 2) * 8 + y * 2 + c
    intra = x * 2 + z // 2
    return inter * 8 + intra


def permutation(move):
    pairs = []
    for x in range(4):
        for y in range(4):
            for z in range(4):
                for c in range(2):
                    a, b, d, e = move(x, y, z, c)
                    pairs.append((device(x, y, z, c), device(a % 4, b % 4, d % 4, e)))
    return sorted(pairs)


def send(value, move):
    return lax.ppermute(value, AXES, permutation(move))


def sibling(x, y, z, c):
    return x, y, z, 1 - c


def along_z(sign):
    def move(x, y, z, c):
        return x, y, z + (sign if c == 0 else -sign), c

    return move


def two_z(x, y, z, c):
    return x, y, z + 2, c


def along_first(sign):
    def move(x, y, z, c):
        return (x + sign, y, z, c) if c == 0 else (x, y + sign, z, c)

    return move


def along_second(sign):
    def move(x, y, z, c):
        return (x, y + sign, z, c) if c == 0 else (x + sign, y, z, c)

    return move


def pack(where, cotangent):
    tokens, hidden = cotangent.shape
    piece = hidden // 16

    def kernel(where_ref, *refs):
        for source, target in zip(refs[:4], refs[4:]):
            target[...] = source[...]

    def source_map(step):
        def index(g, w):
            sign = 1 - 2 * w[3]
            offset = {0: 0, 1: sign, 2: -sign, 3: 2}[step]
            return 0, g * 4 + lax.rem(w[2] + offset + 4, 4)

        return index

    block = (tokens, piece)
    return pl.pallas_call(
        kernel,
        grid_spec=pltpu.PrefetchScalarGridSpec(
            num_scalar_prefetch=1,
            grid=(4,),
            in_specs=[pl.BlockSpec(block, source_map(step)) for step in range(4)],
            out_specs=[pl.BlockSpec(block, lambda g, w: (0, g))] * 4,
        ),
        out_shape=[jax.ShapeDtypeStruct((tokens, hidden // 4), cotangent.dtype)] * 4,
        name="pack_cotangent",
    )(where, *([cotangent] * 4))


def partial_sums(where, mine, other, inputs):
    tokens, rows = mine[0].shape
    width = inputs[0].shape[1]
    piece = rows // 4
    unit = piece // 8
    tile = 256

    def kernel(where_ref, *refs):
        own_refs, other_refs, input_refs = refs[:4], refs[4:8], refs[8:12]
        plus_ref, minus_ref, first_ref, third_ref, keep_ref = refs[12:17]
        held, turned, total = refs[17:]
        g = pl.program_id(0)

        @pl.when(g == 0)
        def _():
            for step in range(4):
                held[pl.ds(step * 2 * tokens, 2 * tokens), :] = input_refs[step][...]

        for step in range(4):
            both = jnp.concatenate([own_refs[step][...], other_refs[step][...]], axis=0)
            turned[:, pl.ds(step * 2 * tokens, 2 * tokens)] = both.T

        @pl.loop(0, width // tile)
        def _(column):
            at = pl.ds(pl.multiple_of(column * tile, tile), tile)
            total[:, at] = jnp.dot(
                turned[...], held[:, at], preferred_element_type=jnp.float32
            ).astype(jnp.bfloat16)

        x, y, c = where_ref[0], where_ref[1], where_ref[3]
        step_x = lax.rem(g - x + 4, 4)
        for to_y in range(4):
            step_y = lax.rem(to_y - y + 4, 4)
            first = jnp.where(c == 0, step_x, step_y)
            second = jnp.where(c == 0, step_y, step_x)
            for half in range(2):
                start = (to_y * 2 + half) * unit
                places = {
                    0: (keep_ref, half),
                    1: (first_ref, None) if half == 0 else (plus_ref, 1),
                    2: (plus_ref, 0) if half == 0 else (minus_ref, 0),
                    3: (minus_ref, 1) if half == 0 else (third_ref, None),
                }
                for distance, (ref, slot) in places.items():

                    @pl.when(first == distance)
                    def _(ref=ref, slot=slot, start=start, second=second):
                        value = total[pl.ds(start, unit), :]
                        if slot is None:
                            ref[second] = value
                        else:
                            ref[slot, second] = value

    def whole(shape):
        return pl.BlockSpec(shape, lambda g, w: (0,) * len(shape))

    two, one = (2, 4, unit, width), (4, unit, width)
    shapes = (two, two, one, one, two)
    flops = 2 * 8 * tokens * rows * width
    return pl.pallas_call(
        kernel,
        grid_spec=pltpu.PrefetchScalarGridSpec(
            num_scalar_prefetch=1,
            grid=(4,),
            in_specs=[pl.BlockSpec((tokens, piece), lambda g, w: (0, g))] * 8
            + [whole(value.shape) for value in inputs],
            out_specs=[whole(shape) for shape in shapes],
            scratch_shapes=[
                pltpu.VMEM((8 * tokens, width), jnp.bfloat16),
                pltpu.VMEM((piece, 8 * tokens), jnp.bfloat16),
                pltpu.VMEM((piece, width), jnp.bfloat16),
            ],
        ),
        out_shape=[jax.ShapeDtypeStruct(shape, jnp.bfloat16) for shape in shapes],
        compiler_params=pltpu.CompilerParams(vmem_limit_bytes=48 * 1024 * 1024),
        cost_estimate=pl.CostEstimate(
            flops=flops, bytes_accessed=8 * tokens * (rows + width) * 2 + rows * width * 2, transcendentals=0
        ),
        name="partial_sums",
    )(where, *mine, *other, *inputs)


def wide(value):
    return value.astype(jnp.float32)


def narrow(value):
    return value.astype(jnp.bfloat16)


def ring_sum(plus, minus, first, third, keep, along):
    from_left = send(plus, along(1))
    from_right = send(minus, along(-1))
    left = send(narrow(wide(first) + wide(from_left[0])), along(1))
    right = send(narrow(wide(third) + wide(from_right[0])), along(-1))
    low = wide(keep[0]) + wide(from_right[1]) + wide(left)
    high = wide(keep[1]) + wide(from_left[1]) + wide(right)
    return low, high


def reduce_scatter(plus, minus, first, third, keep):
    low, high = ring_sum(plus, minus, first, third, keep, along_first)
    low, high = narrow(low), narrow(high)
    low, high = ring_sum(
        jnp.stack([low[2], high[1]]),
        jnp.stack([high[2], low[3]]),
        low[1],
        high[3],
        jnp.stack([low[0], high[0]]),
        along_second,
    )
    return narrow(low), narrow(high)


def adamw(grad, master, first_moment, second_moment):
    new_first = 0.9 * first_moment + 0.1 * grad
    new_second = 0.95 * second_moment + 0.05 * (grad * grad)
    first_hat = new_first / (1.0 - 0.9**10)
    second_hat = new_second / (1.0 - 0.95**10)
    step_dir = first_hat / (jnp.sqrt(second_hat) + 1e-08) + 0.1 * master
    new_master = master - 0.02 * step_dir
    return (new_master, new_first, new_second)


def body(layer_input, up_cotangent, master, first_moment, second_moment):
    tokens, columns = layer_input.shape
    total_tokens = tokens * 128
    inter, intra = lax.axis_index("inter"), lax.axis_index("intra")
    c = inter % 2
    x, y, z = intra // 2, (inter // 2) % 4, (intra % 2) * 2 + inter // 8
    where = jnp.stack([x, y, z, c]).astype(jnp.int32)
    half = columns // 2

    low, high = layer_input[:, :half], layer_input[:, half:]
    kept = jnp.where(c == 0, low, high)
    given = jnp.where(c == 0, high, low)
    chip_input = jnp.concatenate([kept, send(given, sibling)], axis=0)

    blocks = pack(where, up_cotangent)
    mine = [
        blocks[0],
        send(blocks[1], along_z(1)),
        send(blocks[2], along_z(-1)),
        send(blocks[3], two_z),
    ]
    other = [send(mine[step], sibling) for step in (0, 2, 1, 3)]

    grads, copies = [], []
    start = 0
    scale = 1.0 / math.sqrt(total_tokens)
    for width in WIDTHS:
        own = chip_input[:, start : start + width]
        near = send(own, along_z(1))
        far = send(own, along_z(-1))
        last = send(near, along_z(1))
        pieces = partial_sums(where, mine, other, [own, near, far, last])
        low, high = reduce_scatter(*pieces)
        ours = jnp.where(c == 0, low, high)
        theirs = send(jnp.where(c == 0, high, low), sibling)
        grad = wide(jnp.concatenate([jnp.where(c == 0, ours, theirs), jnp.where(c == 0, theirs, ours)], axis=1)) * scale
        grads.append(grad)

        def part(value):
            return jnp.concatenate(
                [value[:, start : start + width], value[:, half + start : half + start + width]], axis=1
            )

        fresh = narrow(adamw(grad, part(master), part(first_moment), part(second_moment))[0])
        copies.append(lax.all_gather(fresh, "inter", axis=0, tiled=True))
        start += width

    def joined(parts):
        return jnp.concatenate(
            [part[:, :width] for part, width in zip(parts, WIDTHS)]
            + [part[:, width:] for part, width in zip(parts, WIDTHS)],
            axis=1,
        )

    new_master, new_first, new_second = adamw(joined(grads), master, first_moment, second_moment)
    return (new_master, new_first, new_second, joined(copies))


def solution(mesh):
    in_specs = (
        P(("inter", "intra"), None),
        P(("inter", "intra"), None),
        P(("intra", "inter"), None),
        P(("intra", "inter"), None),
        P(("intra", "inter"), None),
    )
    out_specs = (
        P(("intra", "inter"), None),
        P(("intra", "inter"), None),
        P(("intra", "inter"), None),
        P("intra", None),
    )
    return jax.shard_map(body, mesh=mesh, in_specs=in_specs, out_specs=out_specs, check_vma=False)
```

```python
import functools
import math

import jax
import jax.numpy as jnp
from jax import lax
from jax.experimental import pallas as pl
from jax.experimental.pallas import tpu as pltpu
from jax.sharding import PartitionSpec as P

AXES = ("inter", "intra")
WIDTHS = (512, 1280)


def device(x, y, z, c):
    inter = (z % 2) * 8 + y * 2 + c
    intra = x * 2 + z // 2
    return inter * 8 + intra


def permutation(move):
    pairs = []
    for x in range(4):
        for y in range(4):
            for z in range(4):
                for c in range(2):
                    a, b, d, e = move(x, y, z, c)
                    pairs.append((device(x, y, z, c), device(a % 4, b % 4, d % 4, e)))
    return sorted(pairs)


def send(value, move):
    return lax.ppermute(value, AXES, permutation(move))


def sibling(x, y, z, c):
    return x, y, z, 1 - c


def along_rows(step):
    def move(x, y, z, c):
        return (x, y, z + step, c) if c == 0 else (x + step, y, z, c)

    return move


def along_sums(step):
    def move(x, y, z, c):
        return (x + step, y, z, c) if c == 0 else (x, y, z + step, c)

    return move


def along_y(step):
    def move(x, y, z, c):
        return x, y + step, z, c

    return move


def pack(where, mine, other, steps):
    tokens, hidden = mine.shape
    piece = hidden // 16
    count = len(steps)

    def kernel(where_ref, *refs):
        for place in range(count):
            target = refs[2 * count + place]
            target[:tokens, :] = refs[place][...]
            target[tokens:, :] = refs[count + place][...]

    def source_map(step):
        def index(g, w):
            at = lax.rem(w[0] + step, 4)
            return 0, jnp.where(w[3] == 0, g * 4 + at, at * 4 + g)

        return index

    maps = [pl.BlockSpec((tokens, piece), source_map(step)) for step in steps]
    return pl.pallas_call(
        kernel,
        grid_spec=pltpu.PrefetchScalarGridSpec(
            num_scalar_prefetch=1,
            grid=(4,),
            in_specs=maps + maps,
            out_specs=[pl.BlockSpec((2 * tokens, piece), lambda g, w: (0, g))] * count,
        ),
        out_shape=[jax.ShapeDtypeStruct((2 * tokens, hidden // 4), mine.dtype)] * count,
        cost_estimate=pl.CostEstimate(
            flops=0, bytes_accessed=count * 2 * tokens * hidden, transcendentals=0
        ),
        name="pack_cotangent",
    )(where, *([mine] * count), *([other] * count))


def partial_sums(where, blocks, inputs, y_first):
    tokens, rows = blocks[0].shape
    width = inputs[0].shape[1]
    piece = rows // 4
    unit = piece // 8
    tile = 256

    def kernel(where_ref, *refs):
        block_refs, input_refs = refs[:4], refs[4:8]
        plus_ref, minus_ref, first_ref, third_ref, keep_ref = refs[8:13]
        held, turned, total = refs[13:]
        g = pl.program_id(0)

        @pl.when(g == 0)
        def _():
            for step in range(4):
                held[pl.ds(step * tokens, tokens), :] = input_refs[step][...]

        for step in range(4):
            turned[:, pl.ds(step * tokens, tokens)] = block_refs[step][...].T

        @pl.loop(0, width // tile)
        def _(column):
            at = pl.ds(pl.multiple_of(column * tile, tile), tile)
            total[:, at] = jnp.dot(
                turned[...], held[:, at], preferred_element_type=jnp.float32
            ).astype(jnp.bfloat16)

        step_g = lax.rem(g - where_ref[1] + 4, 4)
        for to_y in range(4):
            step_y = lax.rem(to_y - where_ref[2] + 4, 4)
            first, second = (step_y, step_g) if y_first else (step_g, step_y)
            for half in range(2):
                start = (to_y * 2 + half) * unit
                places = {
                    0: (keep_ref, half),
                    1: (first_ref, None) if half == 0 else (plus_ref, 1),
                    2: (plus_ref, 0) if half == 0 else (minus_ref, 0),
                    3: (minus_ref, 1) if half == 0 else (third_ref, None),
                }
                for distance, (ref, slot) in places.items():

                    @pl.when(first == distance)
                    def _(ref=ref, slot=slot, start=start, second=second):
                        value = total[pl.ds(start, unit), :]
                        if slot is None:
                            ref[second] = value
                        else:
                            ref[slot, second] = value

    def whole(shape):
        return pl.BlockSpec(shape, lambda g, w: (0,) * len(shape))

    two, one = (2, 4, unit, width), (4, unit, width)
    shapes = (two, two, one, one, two)
    return pl.pallas_call(
        kernel,
        grid_spec=pltpu.PrefetchScalarGridSpec(
            num_scalar_prefetch=1,
            grid=(4,),
            in_specs=[pl.BlockSpec((tokens, piece), lambda g, w: (0, g))] * 4
            + [whole(value.shape) for value in inputs],
            out_specs=[whole(shape) for shape in shapes],
            scratch_shapes=[
                pltpu.VMEM((4 * tokens, width), jnp.bfloat16),
                pltpu.VMEM((piece, 4 * tokens), jnp.bfloat16),
                pltpu.VMEM((piece, width), jnp.bfloat16),
            ],
        ),
        out_shape=[jax.ShapeDtypeStruct(shape, jnp.bfloat16) for shape in shapes],
        compiler_params=pltpu.CompilerParams(vmem_limit_bytes=48 * 1024 * 1024),
        cost_estimate=pl.CostEstimate(
            flops=2 * 4 * tokens * rows * width,
            bytes_accessed=4 * tokens * (rows + width) * 2 + rows * width * 2,
            transcendentals=0,
        ),
        name="partial_sums",
    )(where, *blocks, *inputs)


def wide(value):
    return value.astype(jnp.float32)


def narrow(value):
    return value.astype(jnp.bfloat16)


def after(value, *others):
    return lax.optimization_barrier((value, others))[0]


def ring_send(plus, minus, along):
    return send(plus, along(1)), send(minus, along(-1))


def ring_turn(first, third, from_left, from_right, along):
    left = send(narrow(wide(first) + wide(from_left[0])), along(1))
    right = send(narrow(wide(third) + wide(from_right[0])), along(-1))
    return left, right


def ring_end(keep, from_left, from_right, left, right):
    low = wide(keep[0]) + wide(from_right[1]) + wide(left)
    high = wide(keep[1]) + wide(from_left[1]) + wide(right)
    return narrow(low), narrow(high)


def second_round(low, high):
    plus, minus = jnp.stack([low[2], high[1]]), jnp.stack([high[2], low[3]])
    return plus, minus, low[1], high[3], jnp.stack([low[0], high[0]])


def adamw(grad, master, first_moment, second_moment):
    new_first = 0.9 * first_moment + 0.1 * grad
    new_second = 0.95 * second_moment + 0.05 * (grad * grad)
    first_hat = new_first / (1.0 - 0.9**10)
    second_hat = new_second / (1.0 - 0.95**10)
    step_dir = first_hat / (jnp.sqrt(second_hat) + 1e-08) + 0.1 * master
    new_master = master - 0.02 * step_dir
    return (new_master, new_first, new_second)


def body(layer_input, up_cotangent, master, first_moment, second_moment):
    tokens, columns = layer_input.shape
    total_tokens = tokens * 128
    inter, intra = lax.axis_index("inter"), lax.axis_index("intra")
    c = inter % 2
    x, y, z = intra // 2, (inter // 2) % 4, (intra % 2) * 2 + inter // 8
    where = jnp.stack([jnp.where(c == 0, z, x), jnp.where(c == 0, x, z), y, c]).astype(jnp.int32)
    half = columns // 2

    low, high = layer_input[:, :half], layer_input[:, half:]
    kept = jnp.where(c == 0, low, high)
    given = jnp.where(c == 0, high, low)
    chip_input = jnp.concatenate([kept, send(given, sibling)], axis=0)
    other = send(up_cotangent, sibling)

    def spread(value):
        return [send(value, along_rows(step)) for step in (1, 3, 2)]

    starts = [sum(WIDTHS[:place]) for place in range(len(WIDTHS))]
    inputs = [chip_input[:, start : start + width] for start, width in zip(starts, WIDTHS)]
    inputs_0 = [inputs[0], *spread(inputs[0])]
    near, far = pack(where, up_cotangent, other, (1, 3))
    own, last = pack(where, up_cotangent, other, (0, 2))
    blocks = [own, send(near, along_rows(1)), send(far, along_rows(3)), send(last, along_rows(2))]
    inputs_1 = [inputs[1], *spread(inputs[1])]

    plus_0, minus_0, first_0, third_0, keep_0 = partial_sums(where, blocks, inputs_0, True)
    sent_0 = ring_send(plus_0, minus_0, along_y)
    pieces_1 = partial_sums(where, blocks, inputs_1, False)
    sent_0, pieces_1 = lax.optimization_barrier((sent_0, pieces_1))
    plus_1, minus_1, first_1, third_1, keep_1 = pieces_1
    sent_1 = ring_send(plus_1, minus_1, along_sums)
    turned_0 = ring_turn(first_0, third_0, *sent_0, along_y)
    next_0 = second_round(*ring_end(keep_0, *sent_0, *turned_0))
    again_0 = ring_send(next_0[0], next_0[1], along_sums)
    turned_1 = ring_turn(first_1, third_1, *sent_1, along_sums)
    last_0 = ring_turn(next_0[2], next_0[3], *again_0, along_sums)
    summed_0 = ring_end(next_0[4], *again_0, *last_0)
    next_1 = second_round(*ring_end(keep_1, *sent_1, *turned_1))
    again_1 = ring_send(next_1[0], next_1[1], along_y)
    last_1 = ring_turn(next_1[2], next_1[3], *again_1, along_y)
    summed_1 = ring_end(next_1[4], *again_1, *last_1)

    scale = 1.0 / math.sqrt(total_tokens)
    grads, copies = [], []
    for (low, high), start, width in zip((summed_0, summed_1), starts, WIDTHS):
        ours = jnp.where(c == 0, low, high)
        theirs = send(jnp.where(c == 0, high, low), sibling)
        grad = wide(jnp.concatenate([jnp.where(c == 0, ours, theirs), jnp.where(c == 0, theirs, ours)], axis=1)) * scale
        grads.append(grad)

        def part(value):
            return jnp.concatenate(
                [value[:, start : start + width], value[:, half + start : half + start + width]], axis=1
            )

        fresh = narrow(adamw(grad, part(master), part(first_moment), part(second_moment))[0])
        copies.append(lax.all_gather(fresh, "inter", axis=0, tiled=True))

    def joined(parts):
        return jnp.concatenate(
            [part[:, :width] for part, width in zip(parts, WIDTHS)]
            + [part[:, width:] for part, width in zip(parts, WIDTHS)],
            axis=1,
        )

    new_master, new_first, new_second = adamw(joined(grads), master, first_moment, second_moment)
    return (new_master, new_first, new_second, joined(copies))


def solution(mesh):
    in_specs = (
        P(("inter", "intra"), None),
        P(("inter", "intra"), None),
        P(("intra", "inter"), None),
        P(("intra", "inter"), None),
        P(("intra", "inter"), None),
    )
    out_specs = (
        P(("intra", "inter"), None),
        P(("intra", "inter"), None),
        P(("intra", "inter"), None),
        P("intra", None),
    )
    return jax.shard_map(body, mesh=mesh, in_specs=in_specs, out_specs=out_specs, check_vma=False)
```

```python
import functools
import math

import jax
import jax.numpy as jnp
from jax import lax
from jax.experimental import pallas as pl
from jax.experimental.pallas import tpu as pltpu
from jax.sharding import PartitionSpec as P

AXES = ("inter", "intra")
WIDTHS = (768, 1024)


def device(x, y, z, c):
    inter = (z % 2) * 8 + y * 2 + c
    intra = x * 2 + z // 2
    return inter * 8 + intra


def permutation(move):
    pairs = []
    for x in range(4):
        for y in range(4):
            for z in range(4):
                for c in range(2):
                    a, b, d, e = move(x, y, z, c)
                    pairs.append((device(x, y, z, c), device(a % 4, b % 4, d % 4, e)))
    return sorted(pairs)


def send(value, move):
    return lax.ppermute(value, AXES, permutation(move))


def sibling(x, y, z, c):
    return x, y, z, 1 - c


def along_rows(step):
    def move(x, y, z, c):
        return (x, y, z + step, c) if c == 0 else (x + step, y, z, c)

    return move


def along_sums(step):
    def move(x, y, z, c):
        return (x + step, y, z, c) if c == 0 else (x, y, z + step, c)

    return move


def along_y(step):
    def move(x, y, z, c):
        return x, y + step, z, c

    return move


def pack(where, mine, other, steps):
    tokens, hidden = mine.shape
    piece = hidden // 16
    count = len(steps)

    def kernel(where_ref, *refs):
        for place in range(count):
            both = jnp.concatenate([refs[place][...], refs[count + place][...]], axis=0)
            refs[2 * count + place][...] = both.T

    def source_map(step):
        def index(g, w):
            at = lax.rem(w[0] + step, 4)
            return 0, jnp.where(w[3] == 0, g * 4 + at, at * 4 + g)

        return index

    maps = [pl.BlockSpec((tokens, piece), source_map(step)) for step in steps]
    return pl.pallas_call(
        kernel,
        grid_spec=pltpu.PrefetchScalarGridSpec(
            num_scalar_prefetch=1,
            grid=(4,),
            in_specs=maps + maps,
            out_specs=[pl.BlockSpec((piece, 2 * tokens), lambda g, w: (g, 0))] * count,
        ),
        out_shape=[jax.ShapeDtypeStruct((hidden // 4, 2 * tokens), mine.dtype)] * count,
        cost_estimate=pl.CostEstimate(
            flops=0, bytes_accessed=count * 2 * tokens * hidden, transcendentals=0
        ),
        name="pack_cotangent",
    )(where, *([mine] * count), *([other] * count))


def partial_sums(where, blocks, inputs, y_first):
    rows, tokens = blocks[0].shape
    width = inputs[0].shape[1]
    piece = rows // 4
    unit = piece // 8

    def kernel(where_ref, *refs):
        block_refs, input_refs = refs[:4], refs[4:8]
        out_refs = refs[8:-2]
        held, total = refs[-2:]
        g = pl.program_id(0)

        @pl.when(g == 0)
        def _():
            for step in range(4):
                held[pl.ds(step * tokens, tokens), :] = input_refs[step][...]

        turned = jnp.concatenate([ref[...] for ref in block_refs], axis=1)
        total[...] = jnp.dot(turned, held[...], preferred_element_type=jnp.float32).astype(jnp.bfloat16)

        step_g = lax.rem(g - where_ref[1] + 4, 4)
        if not y_first:
            for distance, ref in enumerate(out_refs):

                @pl.when(step_g == distance)
                def _(ref=ref):
                    for to_y in range(4):
                        ref[lax.rem(to_y - where_ref[2] + 4, 4)] = total[pl.ds(to_y * 2 * unit, 2 * unit), :]

            return
        plus_ref, minus_ref, first_ref, third_ref, keep_ref = out_refs
        for to_y in range(4):
            step_y = lax.rem(to_y - where_ref[2] + 4, 4)
            for half in range(2):
                start = (to_y * 2 + half) * unit
                places = {
                    0: (keep_ref, half),
                    1: (first_ref, None) if half == 0 else (plus_ref, 1),
                    2: (plus_ref, 0) if half == 0 else (minus_ref, 0),
                    3: (minus_ref, 1) if half == 0 else (third_ref, None),
                }
                for distance, (ref, slot) in places.items():

                    @pl.when(step_y == distance)
                    def _(ref=ref, slot=slot, start=start):
                        value = total[pl.ds(start, unit), :]
                        if slot is None:
                            ref[step_g] = value
                        else:
                            ref[slot, step_g] = value

    def whole(shape):
        return pl.BlockSpec(shape, lambda g, w: (0,) * len(shape))

    if y_first:
        two, one = (2, 4, unit, width), (4, unit, width)
        shapes = (two, two, one, one, two)
    else:
        shapes = ((4, 2 * unit, width),) * 4
    return pl.pallas_call(
        kernel,
        grid_spec=pltpu.PrefetchScalarGridSpec(
            num_scalar_prefetch=1,
            grid=(4,),
            in_specs=[pl.BlockSpec((piece, tokens), lambda g, w: (g, 0))] * 4
            + [whole(value.shape) for value in inputs],
            out_specs=[whole(shape) for shape in shapes],
            scratch_shapes=[
                pltpu.VMEM((4 * tokens, width), jnp.bfloat16),
                pltpu.VMEM((piece, width), jnp.bfloat16),
            ],
        ),
        out_shape=[jax.ShapeDtypeStruct(shape, jnp.bfloat16) for shape in shapes],
        compiler_params=pltpu.CompilerParams(vmem_limit_bytes=40 * 1024 * 1024),
        cost_estimate=pl.CostEstimate(
            flops=2 * 4 * tokens * rows * width,
            bytes_accessed=4 * tokens * (rows + width) * 2 + rows * width * 2,
            transcendentals=0,
        ),
        name="partial_sums",
    )(where, *blocks, *inputs)


def wide(value):
    return value.astype(jnp.float32)


def narrow(value):
    return value.astype(jnp.bfloat16)


def after(value, *others):
    return lax.optimization_barrier((value, others))[0]


def ring_send(plus, minus, along):
    return send(plus, along(1)), send(minus, along(-1))


def ring_turn(first, third, from_left, from_right, along):
    left = send(narrow(wide(first) + wide(from_left[0])), along(1))
    right = send(narrow(wide(third) + wide(from_right[0])), along(-1))
    return left, right


def ring_end(keep, from_left, from_right, left, right, place):
    low = wide(keep[0, place]) + wide(from_right[1, place]) + wide(left[place])
    high = wide(keep[1, place]) + wide(from_left[1, place]) + wide(right[place])
    return narrow(jnp.concatenate([low, high], axis=0))


def direct(pieces, along):
    return [pieces[0]] + [send(pieces[step], along(step)) for step in (1, 3, 2)]


def summed(received, place=None):
    return narrow(sum(wide(value if place is None else value[place]) for value in received))


def near_and_pair(first, second):
    def move(x, y, z, c):
        steps = first if c == 0 else second
        return (x, y, z ^ 1, c) if steps is None else (x, y + steps, z, c)

    return move


def gather_rows(value, c):
    def choose(low, high):
        return jnp.where(c == 0, low, high)

    one = send(value, near_and_pair(1, None))
    two = send(value, near_and_pair(-1, 1))
    three = send(value, near_and_pair(2, -1))
    four = send(value, near_and_pair(None, 2))
    five = send(one, near_and_pair(None, 1))
    six = send(choose(two, one), near_and_pair(None, -1))
    seven = send(choose(three, one), near_and_pair(None, 2))
    own = [value, one, two, three, four, five, six, seven]
    swapped = [send(part, sibling) for part in own]
    y_steps = jnp.where(c == 0, jnp.array([0, 3, 1, 2, 0, 3, 1, 2]), jnp.array([0, 0, 3, 1, 2, 3, 1, 2]))
    z_steps = jnp.where(c == 0, jnp.array([0, 0, 0, 0, 1, 1, 1, 1]), jnp.array([0, 1, 0, 0, 0, 1, 1, 1]))
    other_y = jnp.where(c == 1, jnp.array([0, 3, 1, 2, 0, 3, 1, 2]), jnp.array([0, 0, 3, 1, 2, 3, 1, 2]))
    other_z = jnp.where(c == 1, jnp.array([0, 0, 0, 0, 1, 1, 1, 1]), jnp.array([0, 1, 0, 0, 0, 1, 1, 1]))
    return own + swapped, jnp.concatenate([y_steps, other_y]), jnp.concatenate([z_steps, other_z])


def assemble(places, gathered, parts, columns):
    rows, first = gathered.shape
    unit, second = parts[0].shape
    first, second, half = first // 2, second // 2, columns // 2

    def kernel(places_ref, gathered_ref, *refs):
        part_refs, out_ref, semaphores = refs[:-2], refs[-2], refs[-1]
        copies = []
        for side in range(2):
            copies.append((gathered_ref.at[:, pl.ds(side * first, first)], out_ref.at[:, pl.ds(side * half, first)]))
            for place, ref in enumerate(part_refs):
                start = pl.multiple_of(places_ref[place] * unit, unit)
                copies.append(
                    (
                        ref.at[:, pl.ds(side * second, second)],
                        out_ref.at[pl.ds(start, unit), pl.ds(side * half + first, second)],
                    )
                )
        copies = [
            pltpu.make_async_copy(source, target, semaphores.at[place]) for place, (source, target) in enumerate(copies)
        ]
        for copy in copies:
            copy.start()
        for copy in copies:
            copy.wait()

    anywhere = pl.BlockSpec(memory_space=pl.ANY)
    return pl.pallas_call(
        kernel,
        grid_spec=pltpu.PrefetchScalarGridSpec(
            num_scalar_prefetch=1,
            grid=(1,),
            in_specs=[anywhere] * (1 + len(parts)),
            out_specs=anywhere,
            scratch_shapes=[pltpu.SemaphoreType.DMA((2 * (1 + len(parts)),))],
        ),
        out_shape=jax.ShapeDtypeStruct((rows, columns), jnp.bfloat16),
        name="assemble_copy",
    )(places, gathered, *parts)


def adamw(grad, master, first_moment, second_moment):
    new_first = 0.9 * first_moment + 0.1 * grad
    new_second = 0.95 * second_moment + 0.05 * (grad * grad)
    first_hat = new_first / (1.0 - 0.9**10)
    second_hat = new_second / (1.0 - 0.95**10)
    step_dir = first_hat / (jnp.sqrt(second_hat) + 1e-08) + 0.1 * master
    new_master = master - 0.02 * step_dir
    return (new_master, new_first, new_second)


def body(layer_input, up_cotangent, master, first_moment, second_moment):
    tokens, columns = layer_input.shape
    total_tokens = tokens * 128
    inter, intra = lax.axis_index("inter"), lax.axis_index("intra")
    c = inter % 2
    x, y, z = intra // 2, (inter // 2) % 4, (intra % 2) * 2 + inter // 8
    where = jnp.stack([jnp.where(c == 0, z, x), jnp.where(c == 0, x, z), y, c]).astype(jnp.int32)
    half = columns // 2

    low, high = layer_input[:, :half], layer_input[:, half:]
    kept = jnp.where(c == 0, low, high)
    given = jnp.where(c == 0, high, low)
    chip_input = jnp.concatenate([kept, send(given, sibling)], axis=0)
    other = send(after(up_cotangent, given), sibling)

    def spread(value):
        return [send(value, along_rows(step)) for step in (1, 3, 2)]

    starts = [sum(WIDTHS[:place]) for place in range(len(WIDTHS))]
    inputs = [chip_input[:, start : start + width] for start, width in zip(starts, WIDTHS)]
    inputs_0 = [inputs[0], *spread(inputs[0])]
    near, far = pack(where, up_cotangent, other, (1, 3))
    near, far = after((near, far), inputs_0)
    own, last = pack(after(where, near), up_cotangent, other, (0, 2))
    blocks = [own, send(near, along_rows(1)), send(far, along_rows(3)), send(last, along_rows(2))]
    inputs_1 = [inputs[1], *spread(after(inputs[1], blocks))]

    plus, minus, first, third, keep = partial_sums(where, blocks, inputs_0, True)
    sent_0 = ring_send(plus, minus, along_y)
    pieces_1 = partial_sums(where, blocks, inputs_1, False)
    sent_0, pieces_1 = lax.optimization_barrier((sent_0, pieces_1))
    sent_1 = direct(pieces_1, along_sums)
    turned_0 = ring_turn(first, third, *sent_0, along_y)
    again_0 = direct([ring_end(keep, *sent_0, *turned_0, place) for place in range(4)], along_sums)
    again_1 = direct([summed(sent_1, place) for place in range(4)], along_y)

    scale = 1.0 / math.sqrt(total_tokens)
    grads, copies = [], []
    for rows, start, width in zip((summed(again_0), summed(again_1)), starts, WIDTHS):
        low, high = rows[: rows.shape[0] // 2], rows[rows.shape[0] // 2 :]
        ours = jnp.where(c == 0, low, high)
        theirs = send(jnp.where(c == 0, high, low), sibling)
        grad = wide(jnp.concatenate([jnp.where(c == 0, ours, theirs), jnp.where(c == 0, theirs, ours)], axis=1)) * scale
        grads.append(grad)

        def part(value):
            return jnp.concatenate(
                [value[:, start : start + width], value[:, half + start : half + start + width]], axis=1
            )

        copies.append(narrow(adamw(grad, part(master), part(first_moment), part(second_moment))[0]))

    def joined(parts):
        return jnp.concatenate(
            [part[:, :width] for part, width in zip(parts, WIDTHS)]
            + [part[:, width:] for part, width in zip(parts, WIDTHS)],
            axis=1,
        )

    gathered = lax.all_gather(copies[0], "inter", axis=0, tiled=True)
    parts, y_steps, z_steps = gather_rows(copies[1], c)
    cores = jnp.array([0] * 8 + [1] * 8)
    places = (((z + z_steps) % 2) * 8 + ((y + y_steps) % 4) * 2 + (c + cores) % 2).astype(jnp.int32)
    new_copy = assemble(places, gathered, parts, columns)
    new_master, new_first, new_second = adamw(joined(grads), master, first_moment, second_moment)
    return (new_master, new_first, new_second, new_copy)


def solution(mesh):
    in_specs = (
        P(("inter", "intra"), None),
        P(("inter", "intra"), None),
        P(("intra", "inter"), None),
        P(("intra", "inter"), None),
        P(("intra", "inter"), None),
    )
    out_specs = (
        P(("intra", "inter"), None),
        P(("intra", "inter"), None),
        P(("intra", "inter"), None),
        P("intra", None),
    )
    return jax.shard_map(body, mesh=mesh, in_specs=in_specs, out_specs=out_specs, check_vma=False)
```

```python
import functools
import math

import jax
import jax.numpy as jnp
from jax import lax
from jax.experimental import pallas as pl
from jax.experimental.pallas import tpu as pltpu
from jax.sharding import PartitionSpec as P

AXES = ("inter", "intra")
WIDTHS = (768, 1024)


def device(x, y, z, c):
    inter = (z % 2) * 8 + y * 2 + c
    intra = x * 2 + z // 2
    return inter * 8 + intra


def permutation(move):
    pairs = []
    for x in range(4):
        for y in range(4):
            for z in range(4):
                for c in range(2):
                    a, b, d, e = move(x, y, z, c)
                    pairs.append((device(x, y, z, c), device(a % 4, b % 4, d % 4, e)))
    return sorted(pairs)


def send(value, move):
    return lax.ppermute(value, AXES, permutation(move))


def sibling(x, y, z, c):
    return x, y, z, 1 - c


def along_rows(step):
    def move(x, y, z, c):
        return (x, y, z + step, c) if c == 0 else (x + step, y, z, c)

    return move


def along_sums(step):
    def move(x, y, z, c):
        return (x + step, y, z, c) if c == 0 else (x, y, z + step, c)

    return move


def along_y(step):
    def move(x, y, z, c):
        return x, y + step, z, c

    return move


def pack(where, mine, other, steps):
    tokens, hidden = mine.shape
    piece = hidden // 16
    count = len(steps)

    def kernel(where_ref, *refs):
        for place in range(count):
            both = jnp.concatenate([refs[place][...], refs[count + place][...]], axis=0)
            refs[2 * count + place][...] = both.T

    def source_map(step):
        def index(g, w):
            at = lax.rem(w[0] + step, 4)
            return 0, jnp.where(w[3] == 0, g * 4 + at, at * 4 + g)

        return index

    maps = [pl.BlockSpec((tokens, piece), source_map(step)) for step in steps]
    return pl.pallas_call(
        kernel,
        grid_spec=pltpu.PrefetchScalarGridSpec(
            num_scalar_prefetch=1,
            grid=(4,),
            in_specs=maps + maps,
            out_specs=[pl.BlockSpec((piece, 2 * tokens), lambda g, w: (g, 0))] * count,
        ),
        out_shape=[jax.ShapeDtypeStruct((hidden // 4, 2 * tokens), mine.dtype)] * count,
        cost_estimate=pl.CostEstimate(
            flops=0, bytes_accessed=count * 2 * tokens * hidden, transcendentals=0
        ),
        name="pack_cotangent",
    )(where, *([mine] * count), *([other] * count))


def partial_sums(where, blocks, inputs, y_first):
    rows, tokens = blocks[0].shape
    width = inputs[0].shape[1]
    piece = rows // 4
    unit = piece // 8

    def kernel(where_ref, *refs):
        block_refs, input_refs = refs[:4], refs[4:8]
        out_refs = refs[8:-2]
        held, total = refs[-2:]
        g = pl.program_id(0)

        @pl.when(g == 0)
        def _():
            for step in range(4):
                held[pl.ds(step * tokens, tokens), :] = input_refs[step][...]

        turned = jnp.concatenate([ref[...] for ref in block_refs], axis=1)
        total[...] = jnp.dot(turned, held[...], preferred_element_type=jnp.float32).astype(jnp.bfloat16)

        step_g = lax.rem(g - where_ref[1] + 4, 4)
        if not y_first:
            for distance, ref in enumerate(out_refs):

                @pl.when(step_g == distance)
                def _(ref=ref):
                    for to_y in range(4):
                        ref[lax.rem(to_y - where_ref[2] + 4, 4)] = total[pl.ds(to_y * 2 * unit, 2 * unit), :]

            return
        plus_ref, minus_ref, first_ref, third_ref, keep_ref = out_refs
        for to_y in range(4):
            step_y = lax.rem(to_y - where_ref[2] + 4, 4)
            for half in range(2):
                start = (to_y * 2 + half) * unit
                places = {
                    0: (keep_ref, half),
                    1: (first_ref, None) if half == 0 else (plus_ref, 1),
                    2: (plus_ref, 0) if half == 0 else (minus_ref, 0),
                    3: (minus_ref, 1) if half == 0 else (third_ref, None),
                }
                for distance, (ref, slot) in places.items():

                    @pl.when(step_y == distance)
                    def _(ref=ref, slot=slot, start=start):
                        value = total[pl.ds(start, unit), :]
                        if slot is None:
                            ref[step_g] = value
                        else:
                            ref[slot, step_g] = value

    def whole(shape):
        return pl.BlockSpec(shape, lambda g, w: (0,) * len(shape))

    if y_first:
        two, one = (2, 4, unit, width), (4, unit, width)
        shapes = (two, two, one, one, two)
    else:
        shapes = ((4, 2 * unit, width),) * 4
    return pl.pallas_call(
        kernel,
        grid_spec=pltpu.PrefetchScalarGridSpec(
            num_scalar_prefetch=1,
            grid=(4,),
            in_specs=[pl.BlockSpec((piece, tokens), lambda g, w: (g, 0))] * 4
            + [whole(value.shape) for value in inputs],
            out_specs=[whole(shape) for shape in shapes],
            scratch_shapes=[
                pltpu.VMEM((4 * tokens, width), jnp.bfloat16),
                pltpu.VMEM((piece, width), jnp.bfloat16),
            ],
        ),
        out_shape=[jax.ShapeDtypeStruct(shape, jnp.bfloat16) for shape in shapes],
        compiler_params=pltpu.CompilerParams(vmem_limit_bytes=40 * 1024 * 1024),
        cost_estimate=pl.CostEstimate(
            flops=2 * 4 * tokens * rows * width,
            bytes_accessed=4 * tokens * (rows + width) * 2 + rows * width * 2,
            transcendentals=0,
        ),
        name="partial_sums",
    )(where, *blocks, *inputs)


def wide(value):
    return value.astype(jnp.float32)


def narrow(value):
    return value.astype(jnp.bfloat16)


def tie(*values):
    return lax.optimization_barrier(values)


def ring_send(plus, minus, along):
    return send(plus, along(1)), send(minus, along(-1))


def ring_turn(first, third, from_left, from_right, along):
    left = send(narrow(wide(first) + wide(from_left[0])), along(1))
    right = send(narrow(wide(third) + wide(from_right[0])), along(-1))
    return left, right


def ring_end(keep, from_left, from_right, left, right, place):
    low = wide(keep[0, place]) + wide(from_right[1, place]) + wide(left[place])
    high = wide(keep[1, place]) + wide(from_left[1, place]) + wide(right[place])
    return narrow(jnp.concatenate([low, high], axis=0))


def direct(pieces, along):
    return [pieces[0]] + [send(pieces[step], along(step)) for step in (1, 3, 2)]


def summed(received, place=None):
    return narrow(sum(wide(value if place is None else value[place]) for value in received))


def near_and_pair(first, second):
    def move(x, y, z, c):
        steps = first if c == 0 else second
        return (x, y, z ^ 1, c) if steps is None else (x, y + steps, z, c)

    return move


def gather_rows(value, c):
    def choose(low, high):
        return jnp.where(c == 0, low, high)

    one = send(value, near_and_pair(1, None))
    two = send(value, near_and_pair(-1, 1))
    three = send(value, near_and_pair(2, -1))
    four = send(value, near_and_pair(None, 2))
    five = send(one, near_and_pair(None, 1))
    six = send(choose(two, one), near_and_pair(None, -1))
    seven = send(choose(three, one), near_and_pair(None, 2))
    own = [value, one, two, three, four, five, six, seven]
    swapped = [send(part, sibling) for part in own]
    y_steps = jnp.where(c == 0, jnp.array([0, 3, 1, 2, 0, 3, 1, 2]), jnp.array([0, 0, 3, 1, 2, 3, 1, 2]))
    z_steps = jnp.where(c == 0, jnp.array([0, 0, 0, 0, 1, 1, 1, 1]), jnp.array([0, 1, 0, 0, 0, 1, 1, 1]))
    other_y = jnp.where(c == 1, jnp.array([0, 3, 1, 2, 0, 3, 1, 2]), jnp.array([0, 0, 3, 1, 2, 3, 1, 2]))
    other_z = jnp.where(c == 1, jnp.array([0, 0, 0, 0, 1, 1, 1, 1]), jnp.array([0, 1, 0, 0, 0, 1, 1, 1]))
    return own + swapped, jnp.concatenate([y_steps, other_y]), jnp.concatenate([z_steps, other_z])


def assemble(places, gathered, parts, columns):
    rows, first = gathered.shape
    unit, second = parts[0].shape
    first, second, half = first // 2, second // 2, columns // 2

    def kernel(places_ref, gathered_ref, *refs):
        out_ref = refs[-1]
        for side in range(2):
            out_ref[:, pl.ds(side * half, first)] = gathered_ref[:, pl.ds(side * first, first)]
        for place, ref in enumerate(refs[:-1]):

            @pl.when(pl.program_id(0) == place)
            def _(ref=ref):
                for side in range(2):
                    out_ref[:, pl.ds(side * half + first, second)] = ref[:, pl.ds(side * second, second)]

    return pl.pallas_call(
        kernel,
        grid_spec=pltpu.PrefetchScalarGridSpec(
            num_scalar_prefetch=1,
            grid=(len(parts),),
            in_specs=[pl.BlockSpec((unit, 2 * first), lambda k, p: (p[k], 0))]
            + [pl.BlockSpec((unit, 2 * second), lambda k, p: (0, 0))] * len(parts),
            out_specs=pl.BlockSpec((unit, columns), lambda k, p: (p[k], 0)),
        ),
        out_shape=jax.ShapeDtypeStruct((rows, columns), jnp.bfloat16),
        compiler_params=pltpu.CompilerParams(vmem_limit_bytes=32 * 1024 * 1024),
        name="assemble_copy",
    )(places, gathered, *parts)


def adamw(grad, master, first_moment, second_moment):
    new_first = 0.9 * first_moment + 0.1 * grad
    new_second = 0.95 * second_moment + 0.05 * (grad * grad)
    first_hat = new_first / (1.0 - 0.9**10)
    second_hat = new_second / (1.0 - 0.95**10)
    step_dir = first_hat / (jnp.sqrt(second_hat) + 1e-08) + 0.1 * master
    new_master = master - 0.02 * step_dir
    return (new_master, new_first, new_second)


def body(layer_input, up_cotangent, master, first_moment, second_moment):
    tokens, columns = layer_input.shape
    total_tokens = tokens * 128
    inter, intra = lax.axis_index("inter"), lax.axis_index("intra")
    c = inter % 2
    x, y, z = intra // 2, (inter // 2) % 4, (intra % 2) * 2 + inter // 8
    where = jnp.stack([jnp.where(c == 0, z, x), jnp.where(c == 0, x, z), y, c]).astype(jnp.int32)
    half = columns // 2

    low, high = layer_input[:, :half], layer_input[:, half:]
    kept = jnp.where(c == 0, low, high)
    given = jnp.where(c == 0, high, low)
    chip_input = jnp.concatenate([kept, send(given, sibling)], axis=0)
    chip_input, swapped = tie(chip_input, up_cotangent)
    other = send(swapped, sibling)

    def spread(value):
        return [send(value, along_rows(step)) for step in (1, 3, 2)]

    starts = [sum(WIDTHS[:place]) for place in range(len(WIDTHS))]
    inputs = [chip_input[:, start : start + width] for start, width in zip(starts, WIDTHS)]
    inputs_0 = [inputs[0], *spread(inputs[0])]
    (last,) = pack(where, up_cotangent, other, (2,))
    last, where = tie(last, where)
    last = send(last, along_rows(2))
    near, far = pack(where, up_cotangent, other, (1, 3))
    near, far, inputs_0, where = tie(near, far, inputs_0, where)
    (own,) = pack(where, up_cotangent, other, (0,))
    blocks = [own, send(near, along_rows(1)), send(far, along_rows(3)), last]
    blocks, waiting = tie(blocks, inputs[1])
    inputs_1 = [inputs[1], *spread(waiting)]

    plus, minus, first, third, keep = partial_sums(where, blocks, inputs_0, True)
    sent_0 = ring_send(plus, minus, along_y)
    pieces_1 = partial_sums(where, blocks, inputs_1, False)
    sent_0, pieces_1 = lax.optimization_barrier((sent_0, pieces_1))
    sent_1 = direct(pieces_1, along_sums)
    turned_0 = ring_turn(first, third, *sent_0, along_y)
    turned_0, sent_1 = tie(turned_0, sent_1)
    again_0 = direct([ring_end(keep, *sent_0, *turned_0, place) for place in range(4)], along_sums)
    again_1 = direct([summed(sent_1, place) for place in range(4)], along_y)

    scale = 1.0 / math.sqrt(total_tokens)
    grads, copies = [], []
    for rows, start, width in zip((summed(again_0), summed(again_1)), starts, WIDTHS):
        low, high = rows[: rows.shape[0] // 2], rows[rows.shape[0] // 2 :]
        ours = jnp.where(c == 0, low, high)
        theirs = send(jnp.where(c == 0, high, low), sibling)
        grad = wide(jnp.concatenate([jnp.where(c == 0, ours, theirs), jnp.where(c == 0, theirs, ours)], axis=1)) * scale
        grads.append(grad)

        def part(value):
            return jnp.concatenate(
                [value[:, start : start + width], value[:, half + start : half + start + width]], axis=1
            )

        copies.append(narrow(adamw(grad, part(master), part(first_moment), part(second_moment))[0]))

    def joined(parts):
        return jnp.concatenate(
            [part[:, :width] for part, width in zip(parts, WIDTHS)]
            + [part[:, width:] for part, width in zip(parts, WIDTHS)],
            axis=1,
        )

    gathered = lax.all_gather(copies[0], "inter", axis=0, tiled=True)
    parts, y_steps, z_steps = gather_rows(copies[1], c)
    cores = jnp.array([0] * 8 + [1] * 8)
    places = (((z + z_steps) % 2) * 8 + ((y + y_steps) % 4) * 2 + (c + cores) % 2).astype(jnp.int32)
    new_copy = assemble(places, gathered, parts, columns)
    new_master, new_first, new_second = adamw(joined(grads), master, first_moment, second_moment)
    return (new_master, new_first, new_second, new_copy)


def solution(mesh):
    in_specs = (
        P(("inter", "intra"), None),
        P(("inter", "intra"), None),
        P(("intra", "inter"), None),
        P(("intra", "inter"), None),
        P(("intra", "inter"), None),
    )
    out_specs = (
        P(("intra", "inter"), None),
        P(("intra", "inter"), None),
        P(("intra", "inter"), None),
        P("intra", None),
    )
    return jax.shard_map(body, mesh=mesh, in_specs=in_specs, out_specs=out_specs, check_vma=False)
```

```python
import functools
import math

import jax
import jax.numpy as jnp
from jax import lax
from jax.experimental import pallas as pl
from jax.experimental.pallas import tpu as pltpu
from jax.sharding import PartitionSpec as P

AXES = ("inter", "intra")
WIDTHS = (768, 1024)


def device(x, y, z, c):
    inter = (z % 2) * 8 + y * 2 + c
    intra = x * 2 + z // 2
    return inter * 8 + intra


def permutation(move):
    pairs = []
    for x in range(4):
        for y in range(4):
            for z in range(4):
                for c in range(2):
                    a, b, d, e = move(x, y, z, c)
                    pairs.append((device(x, y, z, c), device(a % 4, b % 4, d % 4, e)))
    return sorted(pairs)


def send(value, move):
    return lax.ppermute(value, AXES, permutation(move))


def sibling(x, y, z, c):
    return x, y, z, 1 - c


def along_rows(step):
    def move(x, y, z, c):
        return (x, y, z + step, c) if c == 0 else (x + step, y, z, c)

    return move


def along_sums(step):
    def move(x, y, z, c):
        return (x + step, y, z, c) if c == 0 else (x, y, z + step, c)

    return move


def along_y(step):
    def move(x, y, z, c):
        return x, y + step, z, c

    return move


VMEM = pl.BlockSpec(memory_space=pltpu.VMEM)
SMEM = pl.BlockSpec(memory_space=pltpu.SMEM)


def pack(where, mine, other):
    tokens, hidden = mine.shape
    piece = hidden // 16

    def kernel(where_ref, mine_ref, other_ref, *out_refs):
        @pl.loop(0, 4)
        def _(g):
            rows = pl.ds(pl.multiple_of(g * piece, piece), piece)
            for step, out_ref in enumerate(out_refs):
                at = lax.rem(where_ref[0] + step, 4)
                place = jnp.where(where_ref[3] == 0, g * 4 + at, at * 4 + g)
                columns = pl.ds(pl.multiple_of(place * piece, piece), piece)
                both = jnp.concatenate([mine_ref[:, columns], other_ref[:, columns]], axis=0)
                out_ref[rows, :] = both.T

    return pl.pallas_call(
        kernel,
        in_specs=[SMEM, VMEM, VMEM],
        out_specs=[VMEM] * 4,
        out_shape=[jax.ShapeDtypeStruct((hidden // 4, 2 * tokens), mine.dtype)] * 4,
        compiler_params=pltpu.CompilerParams(vmem_limit_bytes=24 * 1024 * 1024),
        cost_estimate=pl.CostEstimate(flops=0, bytes_accessed=8 * tokens * hidden, transcendentals=0),
        name="pack_cotangent",
    )(where, mine, other)


def partial_sums(where, blocks, inputs, y_first):
    rows, tokens = blocks[0].shape
    width = inputs[0].shape[1]
    piece = rows // 4
    unit = piece // 8

    def kernel(where_ref, *refs):
        block_refs, input_refs = refs[:4], refs[4:8]
        out_refs = refs[8:-2]
        held, total = refs[-2:]
        for step in range(4):
            held[pl.ds(step * tokens, tokens), :] = input_refs[step][...]

        @pl.loop(0, 4)
        def _(g):
            at = pl.ds(pl.multiple_of(g * piece, piece), piece)
            turned = jnp.concatenate([ref[at, :] for ref in block_refs], axis=1)
            total[...] = jnp.dot(turned, held[...], preferred_element_type=jnp.float32).astype(jnp.bfloat16)

            step_g = lax.rem(g - where_ref[1] + 4, 4)
            if not y_first:
                for distance, ref in enumerate(out_refs):

                    @pl.when(step_g == distance)
                    def _(ref=ref):
                        for to_y in range(4):
                            ref[lax.rem(to_y - where_ref[2] + 4, 4)] = total[pl.ds(to_y * 2 * unit, 2 * unit), :]

                return
            plus_ref, minus_ref, first_ref, third_ref, keep_ref = out_refs
            for to_y in range(4):
                step_y = lax.rem(to_y - where_ref[2] + 4, 4)
                for half in range(2):
                    start = (to_y * 2 + half) * unit
                    places = {
                        0: (keep_ref, half),
                        1: (first_ref, None) if half == 0 else (plus_ref, 1),
                        2: (plus_ref, 0) if half == 0 else (minus_ref, 0),
                        3: (minus_ref, 1) if half == 0 else (third_ref, None),
                    }
                    for distance, (ref, slot) in places.items():

                        @pl.when(step_y == distance)
                        def _(ref=ref, slot=slot, start=start):
                            value = total[pl.ds(start, unit), :]
                            if slot is None:
                                ref[step_g] = value
                            else:
                                ref[slot, step_g] = value

    if y_first:
        two, one = (2, 4, unit, width), (4, unit, width)
        shapes = (two, two, one, one, two)
    else:
        shapes = ((4, 2 * unit, width),) * 4
    return pl.pallas_call(
        kernel,
        in_specs=[SMEM] + [VMEM] * 8,
        out_specs=[VMEM] * len(shapes),
        scratch_shapes=[
            pltpu.VMEM((4 * tokens, width), jnp.bfloat16),
            pltpu.VMEM((piece, width), jnp.bfloat16),
        ],
        out_shape=[jax.ShapeDtypeStruct(shape, jnp.bfloat16) for shape in shapes],
        compiler_params=pltpu.CompilerParams(vmem_limit_bytes=24 * 1024 * 1024),
        cost_estimate=pl.CostEstimate(
            flops=2 * 4 * tokens * rows * width,
            bytes_accessed=4 * tokens * (rows + width) * 2 + rows * width * 2,
            transcendentals=0,
        ),
        name="partial_sums",
    )(where, *blocks, *inputs)


def wide(value):
    return value.astype(jnp.float32)


def narrow(value):
    return value.astype(jnp.bfloat16)


def tie(*values):
    return lax.optimization_barrier(values)


def ring_send(plus, minus, along):
    return send(plus, along(1)), send(minus, along(-1))


def ring_turn(first, third, from_left, from_right, along):
    left = send(narrow(wide(first) + wide(from_left[0])), along(1))
    right = send(narrow(wide(third) + wide(from_right[0])), along(-1))
    return left, right


def ring_end(keep, from_left, from_right, left, right, place):
    low = wide(keep[0, place]) + wide(from_right[1, place]) + wide(left[place])
    high = wide(keep[1, place]) + wide(from_left[1, place]) + wide(right[place])
    return narrow(jnp.concatenate([low, high], axis=0))


def direct(pieces, along):
    return [pieces[0]] + [send(pieces[step], along(step)) for step in (1, 3, 2)]


def summed(received, place=None):
    return narrow(sum(wide(value if place is None else value[place]) for value in received))


def near_and_pair(first, second):
    def move(x, y, z, c):
        steps = first if c == 0 else second
        return (x, y, z ^ 1, c) if steps is None else (x, y + steps, z, c)

    return move


def gather_rows(value, c, state):
    def choose(low, high):
        return jnp.where(c == 0, low, high)

    one = send(value, near_and_pair(1, None))
    two = send(value, near_and_pair(-1, 1))
    three = send(value, near_and_pair(2, -1))
    four = send(value, near_and_pair(None, 2))
    one, state = tie(one, state)
    five = send(one, near_and_pair(None, 1))
    six = send(choose(two, one), near_and_pair(None, -1))
    seven = send(choose(three, one), near_and_pair(None, 2))
    own = [value, one, two, three, four, five, six, seven]
    swapped = [send(part, sibling) for part in own]
    y_steps = jnp.where(c == 0, jnp.array([0, 3, 1, 2, 0, 3, 1, 2]), jnp.array([0, 0, 3, 1, 2, 3, 1, 2]))
    z_steps = jnp.where(c == 0, jnp.array([0, 0, 0, 0, 1, 1, 1, 1]), jnp.array([0, 1, 0, 0, 0, 1, 1, 1]))
    other_y = jnp.where(c == 1, jnp.array([0, 3, 1, 2, 0, 3, 1, 2]), jnp.array([0, 0, 3, 1, 2, 3, 1, 2]))
    other_z = jnp.where(c == 1, jnp.array([0, 0, 0, 0, 1, 1, 1, 1]), jnp.array([0, 1, 0, 0, 0, 1, 1, 1]))
    steps = jnp.concatenate([y_steps, other_y]), jnp.concatenate([z_steps, other_z])
    return own + swapped, *steps, state


def assemble(places, gathered, parts, columns):
    rows, first = gathered.shape
    unit, second = parts[0].shape
    first, second, half = first // 2, second // 2, columns // 2

    def kernel(places_ref, gathered_ref, *refs):
        part_refs, out_ref, semaphores = refs[:-2], refs[-2], refs[-1]
        copies = []
        for side in range(2):
            copies.append((gathered_ref.at[:, pl.ds(side * first, first)], out_ref.at[:, pl.ds(side * half, first)]))
            for place, ref in enumerate(part_refs):
                start = pl.multiple_of(places_ref[place] * unit, unit)
                copies.append(
                    (
                        ref.at[:, pl.ds(side * second, second)],
                        out_ref.at[pl.ds(start, unit), pl.ds(side * half + first, second)],
                    )
                )
        copies = [
            pltpu.make_async_copy(source, target, semaphores.at[place]) for place, (source, target) in enumerate(copies)
        ]
        for copy in copies:
            copy.start()
        for copy in copies:
            copy.wait()

    return pl.pallas_call(
        kernel,
        in_specs=[SMEM] + [VMEM] * (1 + len(parts)),
        out_specs=pl.BlockSpec(memory_space=pltpu.HBM),
        scratch_shapes=[pltpu.SemaphoreType.DMA((2 * (1 + len(parts)),))],
        out_shape=jax.ShapeDtypeStruct((rows, columns), jnp.bfloat16),
        compiler_params=pltpu.CompilerParams(vmem_limit_bytes=4 * 1024 * 1024),
        name="assemble_copy",
    )(places, gathered, *parts)


def adamw(grad, master, first_moment, second_moment):
    new_first = 0.9 * first_moment + 0.1 * grad
    new_second = 0.95 * second_moment + 0.05 * (grad * grad)
    first_hat = new_first / (1.0 - 0.9**10)
    second_hat = new_second / (1.0 - 0.95**10)
    step_dir = first_hat / (jnp.sqrt(second_hat) + 1e-08) + 0.1 * master
    new_master = master - 0.02 * step_dir
    return (new_master, new_first, new_second)


def body(layer_input, up_cotangent, master, first_moment, second_moment):
    tokens, columns = layer_input.shape
    total_tokens = tokens * 128
    inter, intra = lax.axis_index("inter"), lax.axis_index("intra")
    c = inter % 2
    x, y, z = intra // 2, (inter // 2) % 4, (intra % 2) * 2 + inter // 8
    where = jnp.stack([jnp.where(c == 0, z, x), jnp.where(c == 0, x, z), y, c]).astype(jnp.int32)
    half = columns // 2

    low, high = layer_input[:, :half], layer_input[:, half:]
    kept = jnp.where(c == 0, low, high)
    given = jnp.where(c == 0, high, low)
    chip_input = jnp.concatenate([kept, send(given, sibling)], axis=0)
    chip_input, swapped = tie(chip_input, up_cotangent)
    other = send(swapped, sibling)

    def spread(value):
        return [send(value, along_rows(step)) for step in (1, 3, 2)]

    starts = [sum(WIDTHS[:place]) for place in range(len(WIDTHS))]
    inputs = [chip_input[:, start : start + width] for start, width in zip(starts, WIDTHS)]
    inputs_0 = [inputs[0], *spread(inputs[0])]
    own, near, last, far = pack(where, up_cotangent, other)
    near, far, inputs_0 = tie(near, far, inputs_0)
    blocks = [own, send(near, along_rows(1)), send(far, along_rows(3)), send(last, along_rows(2))]
    blocks, waiting = tie(blocks, inputs[1])
    inputs_1 = [inputs[1], *spread(waiting)]

    plus, minus, first, third, keep = partial_sums(where, blocks, inputs_0, True)
    sent_0 = ring_send(plus, minus, along_y)
    pieces_1 = partial_sums(where, blocks, inputs_1, False)
    sent_0, pieces_1 = lax.optimization_barrier((sent_0, pieces_1))
    sent_1 = direct(pieces_1, along_sums)
    turned_0 = ring_turn(first, third, *sent_0, along_y)
    turned_0, sent_1[1] = tie(turned_0, sent_1[1])
    again_0 = direct([ring_end(keep, *sent_0, *turned_0, place) for place in range(4)], along_sums)
    again_1 = direct([summed(sent_1, place) for place in range(4)], along_y)

    scale = 1.0 / math.sqrt(total_tokens)
    grads, copies = [], []
    for rows, start, width in zip((summed(again_0), summed(again_1)), starts, WIDTHS):
        low, high = rows[: rows.shape[0] // 2], rows[rows.shape[0] // 2 :]
        ours = jnp.where(c == 0, low, high)
        theirs = send(jnp.where(c == 0, high, low), sibling)
        grad = wide(jnp.concatenate([jnp.where(c == 0, ours, theirs), jnp.where(c == 0, theirs, ours)], axis=1)) * scale
        grads.append(grad)

        def part(value):
            return jnp.concatenate(
                [value[:, start : start + width], value[:, half + start : half + start + width]], axis=1
            )

        copies.append(narrow(adamw(grad, part(master), part(first_moment), part(second_moment))[0]))

    def joined(parts):
        return jnp.concatenate(
            [part[:, :width] for part, width in zip(parts, WIDTHS)]
            + [part[:, width:] for part, width in zip(parts, WIDTHS)],
            axis=1,
        )

    state = adamw(joined(grads), master, first_moment, second_moment)
    gathered = lax.all_gather(copies[0], "inter", axis=0, tiled=True)
    parts, y_steps, z_steps, state = gather_rows(copies[1], c, state)
    cores = jnp.array([0] * 8 + [1] * 8)
    places = (((z + z_steps) % 2) * 8 + ((y + y_steps) % 4) * 2 + (c + cores) % 2).astype(jnp.int32)
    return (*state, assemble(places, gathered, parts, columns))


def solution(mesh):
    in_specs = (
        P(("inter", "intra"), None),
        P(("inter", "intra"), None),
        P(("intra", "inter"), None),
        P(("intra", "inter"), None),
        P(("intra", "inter"), None),
    )
    out_specs = (
        P(("intra", "inter"), None),
        P(("intra", "inter"), None),
        P(("intra", "inter"), None),
        P("intra", None),
    )
    return jax.shard_map(body, mesh=mesh, in_specs=in_specs, out_specs=out_specs, check_vma=False)
```

```python
import functools
import math

import jax
import jax.numpy as jnp
from jax import lax
from jax.experimental import pallas as pl
from jax.experimental.pallas import tpu as pltpu
from jax.sharding import PartitionSpec as P

AXES = ("inter", "intra")
WIDTHS = (768, 1024)


def device(x, y, z, c):
    inter = (z % 2) * 8 + y * 2 + c
    intra = x * 2 + z // 2
    return inter * 8 + intra


def permutation(move):
    pairs = []
    for x in range(4):
        for y in range(4):
            for z in range(4):
                for c in range(2):
                    a, b, d, e = move(x, y, z, c)
                    pairs.append((device(x, y, z, c), device(a % 4, b % 4, d % 4, e)))
    return sorted(pairs)


def send(value, move):
    return lax.ppermute(value, AXES, permutation(move))


def sibling(x, y, z, c):
    return x, y, z, 1 - c


def along_rows(step):
    def move(x, y, z, c):
        return (x, y, z + step, c) if c == 0 else (x + step, y, z, c)

    return move


def along_sums(step):
    def move(x, y, z, c):
        return (x + step, y, z, c) if c == 0 else (x, y, z + step, c)

    return move


def along_y(step):
    def move(x, y, z, c):
        return x, y + step, z, c

    return move


VMEM = pl.BlockSpec(memory_space=pltpu.VMEM)
SMEM = pl.BlockSpec(memory_space=pltpu.SMEM)


def pack(where, mine, other):
    tokens, hidden = mine.shape
    piece = hidden // 16

    def kernel(where_ref, mine_ref, other_ref, *out_refs):
        @pl.loop(0, 4)
        def _(g):
            rows = pl.ds(pl.multiple_of(g * piece, piece), piece)
            for step, out_ref in enumerate(out_refs):
                at = lax.rem(where_ref[0] + step, 4)
                place = jnp.where(where_ref[3] == 0, g * 4 + at, at * 4 + g)
                columns = pl.ds(pl.multiple_of(place * piece, piece), piece)
                both = jnp.concatenate([mine_ref[:, columns], other_ref[:, columns]], axis=0)
                out_ref[rows, :] = both.T

    return pl.pallas_call(
        kernel,
        in_specs=[SMEM, VMEM, VMEM],
        out_specs=[VMEM] * 4,
        out_shape=[jax.ShapeDtypeStruct((hidden // 4, 2 * tokens), mine.dtype)] * 4,
        compiler_params=pltpu.CompilerParams(vmem_limit_bytes=24 * 1024 * 1024),
        cost_estimate=pl.CostEstimate(flops=0, bytes_accessed=8 * tokens * hidden, transcendentals=0),
        name="pack_cotangent",
    )(where, mine, other)


def partial_sums(where, blocks, inputs, y_first):
    rows, tokens = blocks[0].shape
    width = inputs[0].shape[1]
    piece = rows // 4
    unit = piece // 8

    def kernel(where_ref, *refs):
        block_refs, input_refs = refs[:4], refs[4:8]
        out_refs = refs[8:-2]
        held, total = refs[-2:]
        for step in range(4):
            held[pl.ds(step * tokens, tokens), :] = input_refs[step][...]

        @pl.loop(0, 4)
        def _(g):
            at = pl.ds(pl.multiple_of(g * piece, piece), piece)
            turned = jnp.concatenate([ref[at, :] for ref in block_refs], axis=1)
            total[...] = jnp.dot(turned, held[...], preferred_element_type=jnp.float32).astype(jnp.bfloat16)

            if not y_first:
                for to_y in range(4):
                    step_y = lax.rem(to_y - where_ref[2] + 4, 4)
                    out_refs[0][g, step_y] = total[pl.ds(to_y * 2 * unit, 2 * unit), :]
                return
            step_g = lax.rem(g - where_ref[1] + 4, 4)
            plus_ref, minus_ref, first_ref, third_ref, keep_ref = out_refs
            for to_y in range(4):
                step_y = lax.rem(to_y - where_ref[2] + 4, 4)
                for half in range(2):
                    start = (to_y * 2 + half) * unit
                    places = {
                        0: (keep_ref, half),
                        1: (first_ref, None) if half == 0 else (plus_ref, 1),
                        2: (plus_ref, 0) if half == 0 else (minus_ref, 0),
                        3: (minus_ref, 1) if half == 0 else (third_ref, None),
                    }
                    for distance, (ref, slot) in places.items():

                        @pl.when(step_y == distance)
                        def _(ref=ref, slot=slot, start=start):
                            value = total[pl.ds(start, unit), :]
                            if slot is None:
                                ref[step_g] = value
                            else:
                                ref[slot, step_g] = value

    if y_first:
        two, one = (2, 4, unit, width), (4, unit, width)
        shapes = (two, two, one, one, two)
    else:
        shapes = ((4, 4, 2 * unit, width),)
    return pl.pallas_call(
        kernel,
        in_specs=[SMEM] + [VMEM] * 8,
        out_specs=[VMEM] * len(shapes),
        scratch_shapes=[
            pltpu.VMEM((4 * tokens, width), jnp.bfloat16),
            pltpu.VMEM((piece, width), jnp.bfloat16),
        ],
        out_shape=[jax.ShapeDtypeStruct(shape, jnp.bfloat16) for shape in shapes],
        compiler_params=pltpu.CompilerParams(vmem_limit_bytes=24 * 1024 * 1024),
        cost_estimate=pl.CostEstimate(
            flops=2 * 4 * tokens * rows * width,
            bytes_accessed=4 * tokens * (rows + width) * 2 + rows * width * 2,
            transcendentals=0,
        ),
        name="partial_sums",
    )(where, *blocks, *inputs)


def wide(value):
    return value.astype(jnp.float32)


def narrow(value):
    return value.astype(jnp.bfloat16)


def tie(*values):
    return lax.optimization_barrier(values)


def ring_send(plus, minus, along):
    return send(plus, along(1)), send(minus, along(-1))


def ring_turn(first, third, from_left, from_right, along):
    left = send(narrow(wide(first) + wide(from_left[0])), along(1))
    right = send(narrow(wide(third) + wide(from_right[0])), along(-1))
    return left, right


def ring_end(keep, from_left, from_right, left, right, place):
    low = wide(keep[0, place]) + wide(from_right[1, place]) + wide(left[place])
    high = wide(keep[1, place]) + wide(from_left[1, place]) + wide(right[place])
    return narrow(jnp.concatenate([low, high], axis=0))


def direct(pieces, along):
    return [pieces[0]] + [send(pieces[step], along(step)) for step in (1, 3, 2)]


def summed(received):
    return narrow(sum(wide(value) for value in received))


def sum_groups():
    groups = [[device(place, y, z, 0) for place in range(4)] for y in range(4) for z in range(4)]
    return groups + [[device(x, y, place, 1) for place in range(4)] for x in range(4) for y in range(4)]


def near_and_pair(first, second):
    def move(x, y, z, c):
        steps = first if c == 0 else second
        return (x, y, z ^ 1, c) if steps is None else (x, y + steps, z, c)

    return move


def gather_rows(value, c, state):
    def choose(low, high):
        return jnp.where(c == 0, low, high)

    one = send(value, near_and_pair(1, None))
    two = send(value, near_and_pair(-1, 1))
    three = send(value, near_and_pair(2, -1))
    four = send(value, near_and_pair(None, 2))
    one, state = tie(one, state)
    five = send(one, near_and_pair(None, 1))
    six = send(choose(two, one), near_and_pair(None, -1))
    seven = send(choose(three, one), near_and_pair(None, 2))
    own = [value, one, two, three, four, five, six, seven]
    swapped = [send(part, sibling) for part in own]
    return own, swapped, state


def gathered_places(y, z, c):
    y_steps = jnp.where(c == 0, jnp.array([0, 3, 1, 2, 0, 3, 1, 2]), jnp.array([0, 0, 3, 1, 2, 3, 1, 2]))
    z_steps = jnp.where(c == 0, jnp.array([0, 0, 0, 0, 1, 1, 1, 1]), jnp.array([0, 1, 0, 0, 0, 1, 1, 1]))
    return (((z + z_steps) % 2) * 8 + ((y + y_steps) % 4) * 2 + c).astype(jnp.int32)


def place_columns(gathered, columns, start):
    rows, width = gathered.shape
    width, half = width // 2, columns // 2

    def kernel(gathered_ref, out_ref, semaphores):
        copies = [
            pltpu.make_async_copy(
                gathered_ref.at[:, pl.ds(side * width, width)],
                out_ref.at[:, pl.ds(side * half + start, width)],
                semaphores.at[side],
            )
            for side in range(2)
        ]
        for copy in copies:
            copy.start()
        for copy in copies:
            copy.wait()

    return pl.pallas_call(
        kernel,
        in_specs=[VMEM],
        out_specs=pl.BlockSpec(memory_space=pltpu.HBM),
        scratch_shapes=[pltpu.SemaphoreType.DMA((2,))],
        out_shape=jax.ShapeDtypeStruct((rows, columns), jnp.bfloat16),
        compiler_params=pltpu.CompilerParams(vmem_limit_bytes=4 * 1024 * 1024),
        name="place_columns",
    )(gathered)


def place_rows(copy, parts, places, start):
    rows, columns = copy.shape
    unit, width = parts[0].shape
    width, half = width // 2, columns // 2

    def kernel(places_ref, copy_ref, *refs):
        part_refs, out_ref, semaphores = refs[:-2], refs[-2], refs[-1]
        copies = []
        for place, ref in enumerate(part_refs):
            at = pl.ds(pl.multiple_of(places_ref[place] * unit, unit), unit)
            for side in range(2):
                copies.append(
                    pltpu.make_async_copy(
                        ref.at[:, pl.ds(side * width, width)],
                        out_ref.at[at, pl.ds(side * half + start, width)],
                        semaphores.at[2 * place + side],
                    )
                )
        for copy in copies:
            copy.start()
        for copy in copies:
            copy.wait()

    hbm = pl.BlockSpec(memory_space=pltpu.HBM)
    return pl.pallas_call(
        kernel,
        in_specs=[SMEM, hbm] + [VMEM] * len(parts),
        out_specs=hbm,
        scratch_shapes=[pltpu.SemaphoreType.DMA((2 * len(parts),))],
        out_shape=jax.ShapeDtypeStruct((rows, columns), jnp.bfloat16),
        input_output_aliases={1: 0},
        compiler_params=pltpu.CompilerParams(vmem_limit_bytes=4 * 1024 * 1024),
        name="place_rows",
    )(places, copy, *parts)


def adamw(grad, master, first_moment, second_moment):
    new_first = 0.9 * first_moment + 0.1 * grad
    new_second = 0.95 * second_moment + 0.05 * (grad * grad)
    first_hat = new_first / (1.0 - 0.9**10)
    second_hat = new_second / (1.0 - 0.95**10)
    step_dir = first_hat / (jnp.sqrt(second_hat) + 1e-08) + 0.1 * master
    new_master = master - 0.02 * step_dir
    return (new_master, new_first, new_second)


def body(layer_input, up_cotangent, master, first_moment, second_moment):
    tokens, columns = layer_input.shape
    total_tokens = tokens * 128
    inter, intra = lax.axis_index("inter"), lax.axis_index("intra")
    c = inter % 2
    x, y, z = intra // 2, (inter // 2) % 4, (intra % 2) * 2 + inter // 8
    where = jnp.stack([jnp.where(c == 0, z, x), jnp.where(c == 0, x, z), y, c]).astype(jnp.int32)
    half = columns // 2

    low, high = layer_input[:, :half], layer_input[:, half:]
    kept = jnp.where(c == 0, low, high)
    given = jnp.where(c == 0, high, low)
    chip_input = jnp.concatenate([kept, send(given, sibling)], axis=0)
    chip_input, swapped = tie(chip_input, up_cotangent)
    other = send(swapped, sibling)

    def spread(value):
        return [send(value, along_rows(step)) for step in (1, 3, 2)]

    starts = [sum(WIDTHS[:place]) for place in range(len(WIDTHS))]
    inputs = [chip_input[:, start : start + width] for start, width in zip(starts, WIDTHS)]
    inputs_0 = [inputs[0], *spread(inputs[0])]
    own, near, last, far = pack(where, up_cotangent, other)
    near, far, inputs_0 = tie(near, far, inputs_0)
    blocks = [own, send(near, along_rows(1)), send(far, along_rows(3)), send(last, along_rows(2))]
    blocks, waiting = tie(blocks, inputs[1])
    inputs_1 = [inputs[1], *spread(waiting)]

    plus, minus, first, third, keep = partial_sums(where, blocks, inputs_0, True)
    sent_0 = ring_send(plus, minus, along_y)
    pieces_1 = partial_sums(where, blocks, inputs_1, False)
    sent_0, pieces_1 = tie(sent_0, pieces_1)
    (part_1,) = lax.psum_scatter(pieces_1[0], AXES, scatter_dimension=0, axis_index_groups=sum_groups(), tiled=True)
    turned_0 = ring_turn(first, third, *sent_0, along_y)
    again_0 = direct([ring_end(keep, *sent_0, *turned_0, place) for place in range(4)], along_sums)
    again_1 = direct([part_1[place] for place in range(4)], along_y)

    scale = 1.0 / math.sqrt(total_tokens)
    grads, copies = [], []
    for rows, start, width in zip((summed(again_0), summed(again_1)), starts, WIDTHS):
        low, high = rows[: rows.shape[0] // 2], rows[rows.shape[0] // 2 :]
        ours = jnp.where(c == 0, low, high)
        theirs = send(jnp.where(c == 0, high, low), sibling)
        grad = wide(jnp.concatenate([jnp.where(c == 0, ours, theirs), jnp.where(c == 0, theirs, ours)], axis=1)) * scale
        grads.append(grad)

        def part(value):
            return jnp.concatenate(
                [value[:, start : start + width], value[:, half + start : half + start + width]], axis=1
            )

        copies.append(narrow(adamw(grad, part(master), part(first_moment), part(second_moment))[0]))

    def joined(parts):
        return jnp.concatenate(
            [part[:, :width] for part, width in zip(parts, WIDTHS)]
            + [part[:, width:] for part, width in zip(parts, WIDTHS)],
            axis=1,
        )

    state = adamw(joined(grads), master, first_moment, second_moment)
    gathered = lax.all_gather(copies[0], "inter", axis=0, tiled=True)
    own_places, other_places = tie(gathered_places(y, z, c), gathered_places(y, z, 1 - c))
    own_parts, other_parts, state = gather_rows(copies[1], c, state)
    new_copy = place_columns(gathered, columns, starts[0])
    new_copy = place_rows(new_copy, own_parts, own_places, starts[1])
    new_copy = place_rows(new_copy, other_parts, other_places, starts[1])
    return (*state, new_copy)


def solution(mesh):
    in_specs = (
        P(("inter", "intra"), None),
        P(("inter", "intra"), None),
        P(("intra", "inter"), None),
        P(("intra", "inter"), None),
        P(("intra", "inter"), None),
    )
    out_specs = (
        P(("intra", "inter"), None),
        P(("intra", "inter"), None),
        P(("intra", "inter"), None),
        P("intra", None),
    )
    return jax.shard_map(body, mesh=mesh, in_specs=in_specs, out_specs=out_specs, check_vma=False)
```

```python
import functools
import math

import jax
import jax.numpy as jnp
from jax import lax
from jax.experimental import pallas as pl
from jax.experimental.pallas import tpu as pltpu
from jax.sharding import PartitionSpec as P

AXES = ("inter", "intra")
WIDTHS = (1024, 768)


def device(x, y, z, c):
    inter = (z % 2) * 8 + y * 2 + c
    intra = x * 2 + z // 2
    return inter * 8 + intra


def permutation(move):
    pairs = []
    for x in range(4):
        for y in range(4):
            for z in range(4):
                for c in range(2):
                    a, b, d, e = move(x, y, z, c)
                    pairs.append((device(x, y, z, c), device(a % 4, b % 4, d % 4, e)))
    return sorted(pairs)


def send(value, move):
    return lax.ppermute(value, AXES, permutation(move))


def sibling(x, y, z, c):
    return x, y, z, 1 - c


def along_rows(step):
    def move(x, y, z, c):
        return (x, y, z + step, c) if c == 0 else (x + step, y, z, c)

    return move


def along_sums(step):
    def move(x, y, z, c):
        return (x + step, y, z, c) if c == 0 else (x, y, z + step, c)

    return move


def along_y(step):
    def move(x, y, z, c):
        return x, y + step, z, c

    return move


def along_rest(step):
    def move(x, y, z, c):
        return (x, y + step, z, c) if c == 0 else (x, y, z + step, c)

    return move


def first_groups():
    groups = [[device(place, y, z, 0) for place in range(4)] for y in range(4) for z in range(4)]
    return groups + [[device(x, place, z, 1) for place in range(4)] for x in range(4) for z in range(4)]


VMEM = pl.BlockSpec(memory_space=pltpu.VMEM)
SMEM = pl.BlockSpec(memory_space=pltpu.SMEM)


def pack(where, mine, other):
    tokens, hidden = mine.shape
    piece = hidden // 16

    def kernel(where_ref, mine_ref, other_ref, *out_refs):
        @pl.loop(0, 4)
        def _(g):
            rows = pl.ds(pl.multiple_of(g * piece, piece), piece)
            for step, out_ref in enumerate(out_refs):
                at = lax.rem(where_ref[0] + step, 4)
                place = jnp.where(where_ref[3] == 0, g * 4 + at, at * 4 + g)
                columns = pl.ds(pl.multiple_of(place * piece, piece), piece)
                both = jnp.concatenate([mine_ref[:, columns], other_ref[:, columns]], axis=0)
                out_ref[rows, :] = both.T

    return pl.pallas_call(
        kernel,
        in_specs=[SMEM, VMEM, VMEM],
        out_specs=[VMEM] * 4,
        out_shape=[jax.ShapeDtypeStruct((hidden // 4, 2 * tokens), mine.dtype)] * 4,
        compiler_params=pltpu.CompilerParams(vmem_limit_bytes=24 * 1024 * 1024),
        cost_estimate=pl.CostEstimate(flops=0, bytes_accessed=8 * tokens * hidden, transcendentals=0),
        name="pack_cotangent",
    )(where, mine, other)


def partial_sums(where, blocks, inputs, ring):
    rows, tokens = blocks[0].shape
    width = inputs[0].shape[1]
    piece = rows // 4
    unit = piece // 8

    def kernel(where_ref, *refs):
        block_refs, input_refs = refs[:4], refs[4:8]
        out_refs, mark_ref = refs[8:-4], refs[-4]
        mark_ref[...] = jnp.zeros_like(mark_ref)
        held, total, semaphores = refs[-3:]
        for step in range(4):
            held[pl.ds(step * tokens, tokens), :] = input_refs[step][...]

        def copies(g, slot):
            step_g = lax.rem(g - where_ref[1] + 4, 4)
            for to_y in range(4):
                step_y = lax.rem(to_y - where_ref[2] + 4, 4)
                first = jnp.where(where_ref[3] == 0, g, to_y)
                second = jnp.where(where_ref[3] == 0, step_y, step_g)
                yield pltpu.make_async_copy(
                    total.at[slot, pl.ds(to_y * 2 * unit, 2 * unit), :],
                    out_refs[0].at[first, second],
                    semaphores.at[slot, to_y],
                )

        for g in range(4):
            slot = g % 2
            if not ring and g >= 2:
                for copy in copies(g - 2, slot):
                    copy.wait()
            turned = jnp.concatenate([ref[pl.ds(g * piece, piece), :] for ref in block_refs], axis=1)
            total[slot] = jnp.dot(turned, held[...], preferred_element_type=jnp.float32).astype(jnp.bfloat16)
            if not ring:
                for copy in copies(g, slot):
                    copy.start()
                continue

            step_g = lax.rem(g - where_ref[1] + 4, 4)
            plus_ref, minus_ref, first_ref, third_ref, keep_ref = out_refs
            places = [
                [(keep_ref, 0), (keep_ref, 1)],
                [(first_ref, None), (plus_ref, 1)],
                [(plus_ref, 0), (minus_ref, 0)],
                [(minus_ref, 1), (third_ref, None)],
            ]
            for distance, halves in enumerate(places):

                @pl.when(step_g == distance)
                def _(halves=halves, slot=slot):
                    for to_y in range(4):
                        step_y = lax.rem(to_y - where_ref[2] + 4, 4)
                        for half, (ref, at) in enumerate(halves):
                            value = total[slot, pl.ds((to_y * 2 + half) * unit, unit), :]
                            if at is None:
                                ref[step_y] = value
                            else:
                                ref[at, step_y] = value

        if not ring:
            for g in (2, 3):
                for copy in copies(g, g % 2):
                    copy.wait()

    if ring:
        two, one = (2, 4, unit, width), (4, unit, width)
        shapes = (two, two, one, one, two)
    else:
        shapes = ((4, 4, 2 * unit, width),)
    return pl.pallas_call(
        kernel,
        in_specs=[SMEM] + [VMEM] * 8,
        out_specs=[VMEM if ring else pl.BlockSpec(memory_space=pltpu.HBM)] * len(shapes) + [VMEM],
        scratch_shapes=[
            pltpu.VMEM((4 * tokens, width), jnp.bfloat16),
            pltpu.VMEM((2, piece, width), jnp.bfloat16),
            pltpu.SemaphoreType.DMA((2, 4)),
        ],
        out_shape=[jax.ShapeDtypeStruct(shape, jnp.bfloat16) for shape in shapes]
        + [jax.ShapeDtypeStruct((8, 128), jnp.float32)],
        compiler_params=pltpu.CompilerParams(vmem_limit_bytes=24 * 1024 * 1024),
        cost_estimate=pl.CostEstimate(
            flops=2 * 4 * tokens * rows * width,
            bytes_accessed=4 * tokens * (rows + width) * 2 + rows * width * 2,
            transcendentals=0,
        ),
        name="partial_sums",
    )(where, *blocks, *inputs)


def wide(value):
    return value.astype(jnp.float32)


def narrow(value):
    return value.astype(jnp.bfloat16)


def tie(*values):
    return lax.optimization_barrier(values)


def ring_send(plus, minus, along):
    return send(plus, along(1)), send(minus, along(-1))


def ring_turn(first, third, from_left, from_right, along):
    left = send(narrow(wide(first) + wide(from_left[0])), along(1))
    right = send(narrow(wide(third) + wide(from_right[0])), along(-1))
    return left, right


def ring_end(keep, from_left, from_right, left, right, place):
    low = wide(keep[0, place]) + wide(from_right[1, place]) + wide(left[place])
    high = wide(keep[1, place]) + wide(from_left[1, place]) + wide(right[place])
    return narrow(jnp.concatenate([low, high], axis=0))


def direct(pieces, along):
    return [pieces[0]] + [send(pieces[step], along(step)) for step in (1, 3, 2)]


def summed(received):
    return narrow(sum(wide(value) for value in received))


def near_and_pair(first, second):
    def move(x, y, z, c):
        steps = first if c == 0 else second
        return (x, y, z ^ 1, c) if steps is None else (x, y + steps, z, c)

    return move


def gather_rows(value, c, state):
    def choose(low, high):
        return jnp.where(c == 0, low, high)

    one = send(value, near_and_pair(1, None))
    two = send(value, near_and_pair(-1, 1))
    three = send(value, near_and_pair(2, -1))
    four = send(value, near_and_pair(None, 2))
    one, state = tie(one, state)
    five = send(one, near_and_pair(None, 1))
    six = send(choose(two, one), near_and_pair(None, -1))
    seven = send(choose(three, one), near_and_pair(None, 2))
    own = [value, one, two, three, four, five, six, seven]
    swapped = [send(part, sibling) for part in own]
    return own, swapped, state


def gathered_places(y, z, c):
    y_steps = jnp.where(c == 0, jnp.array([0, 3, 1, 2, 0, 3, 1, 2]), jnp.array([0, 0, 3, 1, 2, 3, 1, 2]))
    z_steps = jnp.where(c == 0, jnp.array([0, 0, 0, 0, 1, 1, 1, 1]), jnp.array([0, 1, 0, 0, 0, 1, 1, 1]))
    return (((z + z_steps) % 2) * 8 + ((y + y_steps) % 4) * 2 + c).astype(jnp.int32)


def place_columns(gathered, mark, columns, start):
    rows, width = gathered.shape
    width, half = width // 2, columns // 2

    def kernel(gathered_ref, mark_ref, out_ref, semaphores):
        copies = [
            pltpu.make_async_copy(
                gathered_ref.at[:, pl.ds(side * width, width)],
                out_ref.at[:, pl.ds(side * half + start, width)],
                semaphores.at[side],
            )
            for side in range(2)
        ]
        for copy in copies:
            copy.start()
        for copy in copies:
            copy.wait()

    return pl.pallas_call(
        kernel,
        in_specs=[VMEM, pl.BlockSpec(memory_space=pl.ANY)],
        out_specs=pl.BlockSpec(memory_space=pltpu.HBM),
        scratch_shapes=[pltpu.SemaphoreType.DMA((2,))],
        out_shape=jax.ShapeDtypeStruct((rows, columns), jnp.bfloat16),
        compiler_params=pltpu.CompilerParams(vmem_limit_bytes=4 * 1024 * 1024),
        name="place_columns",
    )(gathered, mark)


def place_rows(copy, parts, places, start):
    rows, columns = copy.shape
    unit, width = parts[0].shape
    width, half = width // 2, columns // 2

    def kernel(places_ref, copy_ref, *refs):
        part_refs, out_ref, semaphores = refs[:-2], refs[-2], refs[-1]
        copies = []
        for place, ref in enumerate(part_refs):
            at = pl.ds(pl.multiple_of(places_ref[place] * unit, unit), unit)
            for side in range(2):
                copies.append(
                    pltpu.make_async_copy(
                        ref.at[:, pl.ds(side * width, width)],
                        out_ref.at[at, pl.ds(side * half + start, width)],
                        semaphores.at[2 * place + side],
                    )
                )
        for copy in copies:
            copy.start()
        for copy in copies:
            copy.wait()

    hbm = pl.BlockSpec(memory_space=pltpu.HBM)
    return pl.pallas_call(
        kernel,
        in_specs=[SMEM, hbm] + [VMEM] * len(parts),
        out_specs=hbm,
        scratch_shapes=[pltpu.SemaphoreType.DMA((2 * len(parts),))],
        out_shape=jax.ShapeDtypeStruct((rows, columns), jnp.bfloat16),
        input_output_aliases={1: 0},
        compiler_params=pltpu.CompilerParams(vmem_limit_bytes=4 * 1024 * 1024),
        name="place_rows",
    )(places, copy, *parts)


def adamw(grad, master, first_moment, second_moment):
    new_first = 0.9 * first_moment + 0.1 * grad
    new_second = 0.95 * second_moment + 0.05 * (grad * grad)
    first_hat = new_first / (1.0 - 0.9**10)
    second_hat = new_second / (1.0 - 0.95**10)
    step_dir = first_hat / (jnp.sqrt(second_hat) + 1e-08) + 0.1 * master
    new_master = master - 0.02 * step_dir
    return (new_master, new_first, new_second)


def body(layer_input, up_cotangent, master, first_moment, second_moment):
    tokens, columns = layer_input.shape
    total_tokens = tokens * 128
    inter, intra = lax.axis_index("inter"), lax.axis_index("intra")
    c = inter % 2
    x, y, z = intra // 2, (inter // 2) % 4, (intra % 2) * 2 + inter // 8
    where = jnp.stack([jnp.where(c == 0, z, x), jnp.where(c == 0, x, z), y, c]).astype(jnp.int32)
    half = columns // 2

    low, high = layer_input[:, :half], layer_input[:, half:]
    kept = jnp.where(c == 0, low, high)
    given = jnp.where(c == 0, high, low)
    chip_input = jnp.concatenate([kept, send(given, sibling)], axis=0)
    chip_input, swapped = tie(chip_input, up_cotangent)
    other = send(swapped, sibling)

    def spread(value):
        return [send(value, along_rows(step)) for step in (1, 3, 2)]

    starts = [sum(WIDTHS[:place]) for place in range(len(WIDTHS))]
    inputs = [chip_input[:, start : start + width] for start, width in zip(starts, WIDTHS)]
    inputs_0 = [inputs[0], *spread(inputs[0])]
    own, near, last, far = pack(where, up_cotangent, other)
    near, far, inputs_0 = tie(near, far, inputs_0)
    blocks = [own, send(near, along_rows(1)), send(far, along_rows(3)), send(last, along_rows(2))]
    blocks, waiting = tie(blocks, inputs[1])
    inputs_1 = [inputs[1], *spread(waiting)]

    plus, minus, first, third, keep, _ = partial_sums(where, blocks, inputs_0, True)
    plus, minus, inputs_1[1:] = tie(plus, minus, inputs_1[1:])
    sent_0 = ring_send(plus, minus, along_sums)
    pieces_1, mark = partial_sums(where, blocks, inputs_1, False)
    sent_0, mark = tie(sent_0, mark)
    (part_1,) = lax.psum_scatter(pieces_1, AXES, scatter_dimension=0, axis_index_groups=first_groups(), tiled=True)
    turned_0 = ring_turn(first, third, *sent_0, along_sums)
    again_0 = direct([ring_end(keep, *sent_0, *turned_0, place) for place in range(4)], along_y)
    again_1 = direct([part_1[place] for place in range(4)], along_rest)

    scale = 1.0 / math.sqrt(total_tokens)
    grads, copies = [], []
    for rows, start, width in zip((summed(again_0), summed(again_1)), starts, WIDTHS):
        low, high = rows[: rows.shape[0] // 2], rows[rows.shape[0] // 2 :]
        ours = jnp.where(c == 0, low, high)
        theirs = send(jnp.where(c == 0, high, low), sibling)
        grad = wide(jnp.concatenate([jnp.where(c == 0, ours, theirs), jnp.where(c == 0, theirs, ours)], axis=1)) * scale
        grads.append(grad)

        def part(value):
            return jnp.concatenate(
                [value[:, start : start + width], value[:, half + start : half + start + width]], axis=1
            )

        copies.append(narrow(adamw(grad, part(master), part(first_moment), part(second_moment))[0]))

    def joined(parts):
        return jnp.concatenate(
            [part[:, :width] for part, width in zip(parts, WIDTHS)]
            + [part[:, width:] for part, width in zip(parts, WIDTHS)],
            axis=1,
        )

    state = adamw(joined(grads), master, first_moment, second_moment)
    gathered = lax.all_gather(copies[0], "inter", axis=0, tiled=True)
    own_places, other_places = tie(gathered_places(y, z, c), gathered_places(y, z, 1 - c))
    own_parts, other_parts, state = gather_rows(copies[1], c, state)
    new_copy = place_columns(gathered, mark, columns, starts[0])
    new_copy = place_rows(new_copy, own_parts, own_places, starts[1])
    new_copy = place_rows(new_copy, other_parts, other_places, starts[1])
    return (*state, new_copy)


def solution(mesh):
    in_specs = (
        P(("inter", "intra"), None),
        P(("inter", "intra"), None),
        P(("intra", "inter"), None),
        P(("intra", "inter"), None),
        P(("intra", "inter"), None),
    )
    out_specs = (
        P(("intra", "inter"), None),
        P(("intra", "inter"), None),
        P(("intra", "inter"), None),
        P("intra", None),
    )
    return jax.shard_map(body, mesh=mesh, in_specs=in_specs, out_specs=out_specs, check_vma=False)
```

```python
import functools
import math

import jax
import jax.numpy as jnp
from jax import lax
from jax.experimental import pallas as pl
from jax.experimental.pallas import tpu as pltpu
from jax.sharding import PartitionSpec as P

AXES = ("inter", "intra")
WIDTHS = (1024, 768)


def device(x, y, z, c):
    inter = (z % 2) * 8 + y * 2 + c
    intra = x * 2 + z // 2
    return inter * 8 + intra


def permutation(move):
    pairs = []
    for x in range(4):
        for y in range(4):
            for z in range(4):
                for c in range(2):
                    a, b, d, e = move(x, y, z, c)
                    pairs.append((device(x, y, z, c), device(a % 4, b % 4, d % 4, e)))
    return sorted(pairs)


def send(value, move):
    return lax.ppermute(value, AXES, permutation(move))


def sibling(x, y, z, c):
    return x, y, z, 1 - c


def along_rows(step):
    def move(x, y, z, c):
        return (x, y, z + step, c) if c == 0 else (x + step, y, z, c)

    return move


def along_sums(step):
    def move(x, y, z, c):
        return (x + step, y, z, c) if c == 0 else (x, y, z + step, c)

    return move


def along_y(step):
    def move(x, y, z, c):
        return x, y + step, z, c

    return move


def along_rest(step):
    def move(x, y, z, c):
        return (x, y + step, z, c) if c == 0 else (x, y, z + step, c)

    return move


def row_groups():
    groups = [[device(x, y, place, 0) for place in range(4)] for x in range(4) for y in range(4)]
    return groups + [[device(place, y, z, 1) for place in range(4)] for y in range(4) for z in range(4)]


def first_groups():
    groups = [[device(place, y, z, 0) for place in range(4)] for y in range(4) for z in range(4)]
    return groups + [[device(x, place, z, 1) for place in range(4)] for x in range(4) for z in range(4)]


VMEM = pl.BlockSpec(memory_space=pltpu.VMEM)
SMEM = pl.BlockSpec(memory_space=pltpu.SMEM)


def pack(where, mine, other):
    tokens, hidden = mine.shape
    piece = hidden // 16

    def kernel(where_ref, mine_ref, other_ref, *out_refs):
        @pl.loop(0, 4)
        def _(g):
            rows = pl.ds(pl.multiple_of(g * piece, piece), piece)
            for step, out_ref in enumerate(out_refs):
                at = lax.rem(where_ref[0] + step, 4)
                place = jnp.where(where_ref[3] == 0, g * 4 + at, at * 4 + g)
                columns = pl.ds(pl.multiple_of(place * piece, piece), piece)
                both = jnp.concatenate([mine_ref[:, columns], other_ref[:, columns]], axis=0)
                out_ref[rows, :] = both.T

    return pl.pallas_call(
        kernel,
        in_specs=[SMEM, VMEM, VMEM],
        out_specs=[VMEM] * 4,
        out_shape=[jax.ShapeDtypeStruct((hidden // 4, 2 * tokens), mine.dtype)] * 4,
        compiler_params=pltpu.CompilerParams(vmem_limit_bytes=24 * 1024 * 1024),
        cost_estimate=pl.CostEstimate(flops=0, bytes_accessed=8 * tokens * hidden, transcendentals=0),
        name="pack_cotangent",
    )(where, mine, other)


def partial_sums(where, blocks, inputs, start, width, ring):
    rows, tokens = blocks[0].shape
    piece = rows // 4
    unit = piece // 8

    def kernel(where_ref, *refs):
        block_refs, input_ref = refs[:4], refs[4]
        out_refs = refs[5:-4]
        held, total, semaphores, input_semaphores = refs[-4:]

        loads = []
        for step in range(4):
            at = lax.rem(where_ref[0] + step, 4) * tokens
            source = input_ref.at[pl.ds(pl.multiple_of(at, tokens), tokens), pl.ds(start, width)]
            target = held.at[pl.ds(step * tokens, tokens), :]
            loads.append(pltpu.make_async_copy(source, target, input_semaphores.at[step]))
        for load in loads:
            load.start()
        for load in loads:
            load.wait()

        def copies(g, slot):
            step_g = lax.rem(g - where_ref[1] + 4, 4)
            for to_y in range(4):
                step_y = lax.rem(to_y - where_ref[2] + 4, 4)
                first = jnp.where(where_ref[3] == 0, g, to_y)
                second = jnp.where(where_ref[3] == 0, step_y, step_g)
                yield pltpu.make_async_copy(
                    total.at[slot, pl.ds(to_y * 2 * unit, 2 * unit), :],
                    out_refs[0].at[first, second],
                    semaphores.at[slot, to_y],
                )

        @pl.loop(0, 4)
        def _(g):
            slot = lax.rem(g, 2)
            if not ring:

                @pl.when(g >= 2)
                def _():
                    for copy in copies(g - 2, slot):
                        copy.wait()

            at = pl.ds(pl.multiple_of(g * piece, piece), piece)
            turned = jnp.concatenate([ref[at, :] for ref in block_refs], axis=1)
            total[slot] = jnp.dot(turned, held[...], preferred_element_type=jnp.float32).astype(jnp.bfloat16)
            if not ring:
                for copy in copies(g, slot):
                    copy.start()
                return

            step_g = lax.rem(g - where_ref[1] + 4, 4)
            plus_ref, minus_ref, first_ref, third_ref, keep_ref = out_refs
            places = [
                [(keep_ref, 0), (keep_ref, 1)],
                [(first_ref, None), (plus_ref, 1)],
                [(plus_ref, 0), (minus_ref, 0)],
                [(minus_ref, 1), (third_ref, None)],
            ]
            for distance, halves in enumerate(places):

                @pl.when(step_g == distance)
                def _(halves=halves):
                    for to_y in range(4):
                        step_y = lax.rem(to_y - where_ref[2] + 4, 4)
                        for half, (ref, at) in enumerate(halves):
                            value = total[slot, pl.ds((to_y * 2 + half) * unit, unit), :]
                            if at is None:
                                ref[step_y] = value
                            else:
                                ref[at, step_y] = value

        if not ring:
            for g in (2, 3):
                for copy in copies(g, g % 2):
                    copy.wait()

    hbm = pl.BlockSpec(memory_space=pltpu.HBM)
    if ring:
        two, one = (2, 4, unit, width), (4, unit, width)
        shapes = (two, two, one, one, two)
    else:
        shapes = ((4, 4, 2 * unit, width),)
    return pl.pallas_call(
        kernel,
        in_specs=[SMEM] + [VMEM] * 4 + [hbm],
        out_specs=[VMEM if ring else hbm] * len(shapes),
        scratch_shapes=[
            pltpu.VMEM((4 * tokens, width), jnp.bfloat16),
            pltpu.VMEM((2, piece, width), jnp.bfloat16),
            pltpu.SemaphoreType.DMA((2, 4)),
            pltpu.SemaphoreType.DMA((4,)),
        ],
        out_shape=[jax.ShapeDtypeStruct(shape, jnp.bfloat16) for shape in shapes],
        compiler_params=pltpu.CompilerParams(vmem_limit_bytes=24 * 1024 * 1024),
        cost_estimate=pl.CostEstimate(
            flops=2 * 4 * tokens * rows * width,
            bytes_accessed=4 * tokens * (rows + width) * 2 + rows * width * 2,
            transcendentals=0,
        ),
        name="partial_sums",
    )(where, *blocks, inputs)


def wide(value):
    return value.astype(jnp.float32)


def narrow(value):
    return value.astype(jnp.bfloat16)


def tie(*values):
    return lax.optimization_barrier(values)


def ring_send(plus, minus, along):
    return send(plus, along(1)), send(minus, along(-1))


def ring_turn(first, third, from_left, from_right, along):
    left = send(narrow(wide(first) + wide(from_left[0])), along(1))
    right = send(narrow(wide(third) + wide(from_right[0])), along(-1))
    return left, right


def ring_end(keep, from_left, from_right, left, right, place):
    low = wide(keep[0, place]) + wide(from_right[1, place]) + wide(left[place])
    high = wide(keep[1, place]) + wide(from_left[1, place]) + wide(right[place])
    return narrow(jnp.concatenate([low, high], axis=0))


def direct(pieces, along):
    return [pieces[0]] + [send(pieces[step], along(step)) for step in (1, 3, 2)]


def summed(received):
    return narrow(sum(wide(value) for value in received))


def gather_rows(value):
    def to(y_step, z_bit):
        def move(x, y, z, c):
            return x, y + y_step, z ^ z_bit, c

        return move

    own = [send(value, to(y_step, z_bit)) if y_step or z_bit else value for z_bit in range(2) for y_step in range(4)]
    return own, [send(part, sibling) for part in own]


def gathered_places(y, z, c):
    steps = jnp.arange(8, dtype=jnp.int32)
    return ((z + steps // 4) % 2) * 8 + ((y - steps % 4 + 4) % 4) * 2 + c


def place_columns(gathered, columns, start):
    rows, width = gathered.shape
    width, half = width // 2, columns // 2

    def kernel(gathered_ref, out_ref, semaphores):
        copies = [
            pltpu.make_async_copy(
                gathered_ref.at[:, pl.ds(side * width, width)],
                out_ref.at[:, pl.ds(side * half + start, width)],
                semaphores.at[side],
            )
            for side in range(2)
        ]
        for copy in copies:
            copy.start()
        for copy in copies:
            copy.wait()

    return pl.pallas_call(
        kernel,
        in_specs=[VMEM],
        out_specs=pl.BlockSpec(memory_space=pltpu.HBM),
        scratch_shapes=[pltpu.SemaphoreType.DMA((2,))],
        out_shape=jax.ShapeDtypeStruct((rows, columns), jnp.bfloat16),
        compiler_params=pltpu.CompilerParams(vmem_limit_bytes=4 * 1024 * 1024),
        name="place_columns",
    )(gathered)


def place_rows(copy, parts, places, start):
    rows, columns = copy.shape
    unit, width = parts[0].shape
    width, half = width // 2, columns // 2

    def kernel(places_ref, copy_ref, *refs):
        part_refs, out_ref, semaphores = refs[:-2], refs[-2], refs[-1]
        copies = []
        for place, ref in enumerate(part_refs):
            at = pl.ds(pl.multiple_of(places_ref[place] * unit, unit), unit)
            for side in range(2):
                copies.append(
                    pltpu.make_async_copy(
                        ref.at[:, pl.ds(side * width, width)],
                        out_ref.at[at, pl.ds(side * half + start, width)],
                        semaphores.at[2 * place + side],
                    )
                )
        for copy in copies:
            copy.start()
        for copy in copies:
            copy.wait()

    hbm = pl.BlockSpec(memory_space=pltpu.HBM)
    return pl.pallas_call(
        kernel,
        in_specs=[SMEM, hbm] + [VMEM] * len(parts),
        out_specs=hbm,
        scratch_shapes=[pltpu.SemaphoreType.DMA((2 * len(parts),))],
        out_shape=jax.ShapeDtypeStruct((rows, columns), jnp.bfloat16),
        input_output_aliases={1: 0},
        compiler_params=pltpu.CompilerParams(vmem_limit_bytes=4 * 1024 * 1024),
        name="place_rows",
    )(places, copy, *parts)


def adamw(grad, master, first_moment, second_moment):
    new_first = 0.9 * first_moment + 0.1 * grad
    new_second = 0.95 * second_moment + 0.05 * (grad * grad)
    first_hat = new_first / (1.0 - 0.9**10)
    second_hat = new_second / (1.0 - 0.95**10)
    step_dir = first_hat / (jnp.sqrt(second_hat) + 1e-08) + 0.1 * master
    new_master = master - 0.02 * step_dir
    return (new_master, new_first, new_second)


def body(layer_input, up_cotangent, master, first_moment, second_moment):
    tokens, columns = layer_input.shape
    total_tokens = tokens * 128
    inter, intra = lax.axis_index("inter"), lax.axis_index("intra")
    c = inter % 2
    x, y, z = intra // 2, (inter // 2) % 4, (intra % 2) * 2 + inter // 8
    where = jnp.stack([jnp.where(c == 0, z, x), jnp.where(c == 0, x, z), y, c]).astype(jnp.int32)
    half = columns // 2

    low, high = layer_input[:, :half], layer_input[:, half:]
    kept = jnp.where(c == 0, low, high)
    given = jnp.where(c == 0, high, low)
    chip_input = jnp.concatenate([kept, send(given, sibling)], axis=0)
    chip_input, swapped = tie(chip_input, up_cotangent)
    other = send(swapped, sibling)
    inputs = lax.all_gather(chip_input, AXES, axis=0, axis_index_groups=row_groups(), tiled=True)

    blocks = pack(where, up_cotangent, other)
    blocks = [blocks[0]] + [send(blocks[step], along_rows(step)) for step in (1, 3, 2)]
    blocks = [blocks[0], blocks[2], blocks[3], blocks[1]]

    starts = [sum(WIDTHS[:place]) for place in range(len(WIDTHS))]
    plus, minus, first, third, keep = partial_sums(where, blocks, inputs, starts[0], WIDTHS[0], True)
    sent_0 = ring_send(plus, minus, along_sums)
    pieces_1 = partial_sums(where, blocks, inputs, starts[1], WIDTHS[1], False)
    sent_0, pieces_1 = tie(sent_0, pieces_1)
    (part_1,) = lax.psum_scatter(pieces_1[0], AXES, scatter_dimension=0, axis_index_groups=first_groups(), tiled=True)
    turned_0 = ring_turn(first, third, *sent_0, along_sums)
    again_0 = direct([ring_end(keep, *sent_0, *turned_0, place) for place in range(4)], along_y)
    again_1 = direct([part_1[place] for place in range(4)], along_rest)

    scale = 1.0 / math.sqrt(total_tokens)
    grads, copies = [], []
    for rows, start, width in zip((summed(again_0), summed(again_1)), starts, WIDTHS):
        low, high = rows[: rows.shape[0] // 2], rows[rows.shape[0] // 2 :]
        ours = jnp.where(c == 0, low, high)
        theirs = send(jnp.where(c == 0, high, low), sibling)
        grad = wide(jnp.concatenate([jnp.where(c == 0, ours, theirs), jnp.where(c == 0, theirs, ours)], axis=1)) * scale
        grads.append(grad)

        def part(value):
            return jnp.concatenate(
                [value[:, start : start + width], value[:, half + start : half + start + width]], axis=1
            )

        copies.append(narrow(adamw(grad, part(master), part(first_moment), part(second_moment))[0]))

    def joined(parts):
        return jnp.concatenate(
            [part[:, :width] for part, width in zip(parts, WIDTHS)]
            + [part[:, width:] for part, width in zip(parts, WIDTHS)],
            axis=1,
        )

    state = adamw(joined(grads), master, first_moment, second_moment)
    gathered = lax.all_gather(copies[0], "inter", axis=0, tiled=True)
    own_parts, other_parts = gather_rows(copies[1])
    own_parts[4], state = tie(own_parts[4], state)
    new_copy = place_columns(gathered, columns, starts[0])
    new_copy = place_rows(new_copy, own_parts, gathered_places(y, z, c), starts[1])
    new_copy = place_rows(new_copy, other_parts, gathered_places(y, z, 1 - c), starts[1])
    return (*state, new_copy)


def solution(mesh):
    in_specs = (
        P(("inter", "intra"), None),
        P(("inter", "intra"), None),
        P(("intra", "inter"), None),
        P(("intra", "inter"), None),
        P(("intra", "inter"), None),
    )
    out_specs = (
        P(("intra", "inter"), None),
        P(("intra", "inter"), None),
        P(("intra", "inter"), None),
        P("intra", None),
    )
    return jax.shard_map(body, mesh=mesh, in_specs=in_specs, out_specs=out_specs, check_vma=False)
```

```python
import functools
import math

import jax
import jax.numpy as jnp
from jax import lax
from jax.experimental import pallas as pl
from jax.experimental.pallas import tpu as pltpu
from jax.sharding import PartitionSpec as P

AXES = ("inter", "intra")
WIDTHS = (1024, 768)
SPLIT = 2048


def device(x, y, z, c):
    inter = (z % 2) * 8 + y * 2 + c
    intra = x * 2 + z // 2
    return inter * 8 + intra


def permutation(move):
    pairs = []
    for x in range(4):
        for y in range(4):
            for z in range(4):
                for c in range(2):
                    a, b, d, e = move(x, y, z, c)
                    pairs.append((device(x, y, z, c), device(a % 4, b % 4, d % 4, e)))
    return sorted(pairs)


def send(value, move):
    return lax.ppermute(value, AXES, permutation(move))


def sibling(x, y, z, c):
    return x, y, z, 1 - c


def along_rows(step):
    def move(x, y, z, c):
        return (x, y, z + step, c) if c == 0 else (x + step, y, z, c)

    return move


def along_sums(step):
    def move(x, y, z, c):
        return (x + step, y, z, c) if c == 0 else (x, y, z + step, c)

    return move


def along_y(step):
    def move(x, y, z, c):
        return x, y + step, z, c

    return move


def sum_groups():
    groups = [[device(place, y, z, 0) for place in range(4)] for y in range(4) for z in range(4)]
    return groups + [[device(x, y, place, 1) for place in range(4)] for x in range(4) for y in range(4)]


VMEM = pl.BlockSpec(memory_space=pltpu.VMEM)
SMEM = pl.BlockSpec(memory_space=pltpu.SMEM)


def pack(where, mine, other):
    tokens, hidden = mine.shape
    piece = hidden // 16

    def kernel(where_ref, mine_ref, other_ref, *out_refs):
        @pl.loop(0, 4)
        def _(g):
            rows = pl.ds(pl.multiple_of(g * piece, piece), piece)
            for step, out_ref in enumerate(out_refs):
                at = lax.rem(where_ref[0] + step, 4)
                place = jnp.where(where_ref[3] == 0, g * 4 + at, at * 4 + g)
                columns = pl.ds(pl.multiple_of(place * piece, piece), piece)
                both = jnp.concatenate([mine_ref[:, columns], other_ref[:, columns]], axis=0)
                out_ref[rows, :] = both.T

    return pl.pallas_call(
        kernel,
        in_specs=[SMEM, VMEM, VMEM],
        out_specs=[VMEM] * 4,
        out_shape=[jax.ShapeDtypeStruct((hidden // 4, 2 * tokens), mine.dtype)] * 4,
        compiler_params=pltpu.CompilerParams(vmem_limit_bytes=10 * 1024 * 1024),
        cost_estimate=pl.CostEstimate(flops=0, bytes_accessed=8 * tokens * hidden, transcendentals=0),
        name="pack_cotangent",
    )(where, mine, other)


def partial_sums(where, blocks, inputs, ring):
    rows, tokens = blocks[0].shape
    width = inputs[0].shape[1]
    piece = rows // 4
    unit = piece // 8

    def kernel(where_ref, *refs):
        block_refs, input_refs = refs[:4], refs[4:8]
        out_refs = refs[8:-4]
        held, total, turned, semaphores = refs[-4:]

        def loads(g, slot):
            for step, ref in enumerate(block_refs):
                source = ref.at[pl.ds(pl.multiple_of(g * piece, piece), piece), :]
                target = turned.at[slot, :, pl.ds(step * tokens, tokens)]
                yield pltpu.make_async_copy(source, target, semaphores.at[slot, step])

        for load in loads(0, 0):
            load.start()
        for step in range(4):
            held[pl.ds(step * tokens, tokens), :] = input_refs[step][...]

        @pl.loop(0, 4)
        def _(g):
            slot = lax.rem(g, 2)

            @pl.when(g < 3)
            def _():
                for load in loads(g + 1, 1 - slot):
                    load.start()

            for load in loads(g, slot):
                load.wait()
            total[...] = jnp.dot(turned[slot], held[...], preferred_element_type=jnp.float32).astype(jnp.bfloat16)

            step_g = lax.rem(g - where_ref[1] + 4, 4)
            for to_y in range(4):
                step_y = lax.rem(to_y - where_ref[2] + 4, 4)
                if not ring:
                    out_refs[0][g, step_y] = total[pl.ds(to_y * 2 * unit, 2 * unit), :]
                    continue
                plus_ref, minus_ref, first_ref, third_ref, keep_ref = out_refs
                places = [
                    [(keep_ref, 0), (keep_ref, 1)],
                    [(first_ref, None), (plus_ref, 1)],
                    [(plus_ref, 0), (minus_ref, 0)],
                    [(minus_ref, 1), (third_ref, None)],
                ]
                for distance, halves in enumerate(places):

                    @pl.when(step_y == distance)
                    def _(halves=halves, to_y=to_y):
                        for half, (ref, at) in enumerate(halves):
                            value = total[pl.ds((to_y * 2 + half) * unit, unit), :]
                            if at is None:
                                ref[step_g] = value
                            else:
                                ref[at, step_g] = value

    if ring:
        two, one = (2, 4, unit, width), (4, unit, width)
        shapes = (two, two, one, one, two)
    else:
        shapes = ((4, 4, 2 * unit, width),)
    return pl.pallas_call(
        kernel,
        in_specs=[SMEM] + [pl.BlockSpec(memory_space=pltpu.HBM)] * 4 + [VMEM] * 4,
        out_specs=[VMEM] * len(shapes),
        scratch_shapes=[
            pltpu.VMEM((4 * tokens, width), jnp.bfloat16),
            pltpu.VMEM((piece, width), jnp.bfloat16),
            pltpu.VMEM((2, piece, 4 * tokens), jnp.bfloat16),
            pltpu.SemaphoreType.DMA((2, 4)),
        ],
        out_shape=[jax.ShapeDtypeStruct(shape, jnp.bfloat16) for shape in shapes],
        compiler_params=pltpu.CompilerParams(vmem_limit_bytes=16 * 1024 * 1024),
        cost_estimate=pl.CostEstimate(
            flops=2 * 4 * tokens * rows * width,
            bytes_accessed=4 * tokens * (rows + width) * 2 + rows * width * 2,
            transcendentals=0,
        ),
        name="partial_sums",
    )(where, *[pltpu.with_memory_space_constraint(block, pltpu.HBM) for block in blocks], *inputs)


def wide(value):
    return value.astype(jnp.float32)


def narrow(value):
    return value.astype(jnp.bfloat16)


def tie(*values):
    return lax.optimization_barrier(values)


def ring_send(plus, minus, along):
    return send(plus, along(1)), send(minus, along(-1))


def ring_turn(first, third, from_left, from_right, along):
    left = send(narrow(wide(first) + wide(from_left[0])), along(1))
    right = send(narrow(wide(third) + wide(from_right[0])), along(-1))
    return left, right


def ring_end(keep, from_left, from_right, left, right, place):
    low = wide(keep[0, place]) + wide(from_right[1, place]) + wide(left[place])
    high = wide(keep[1, place]) + wide(from_left[1, place]) + wide(right[place])
    return narrow(jnp.concatenate([low, high], axis=0))


def direct(pieces, along):
    return [pieces[0]] + [send(pieces[step], along(step)) for step in (1, 3, 2)]


def summed(received):
    return narrow(sum(wide(value) for value in received))


def near_and_pair(first, second):
    def move(x, y, z, c):
        steps = first if c == 0 else second
        return (x, y, z ^ 1, c) if steps is None else (x, y + steps, z, c)

    return move


def gather_rows(value, c, grad):
    def choose(low, high):
        return jnp.where(c == 0, low, high)

    one = send(value, near_and_pair(1, None))
    two = send(value, near_and_pair(-1, 1))
    three = send(value, near_and_pair(2, -1))
    four = send(value, near_and_pair(None, 2))
    one, grad = tie(one, grad)
    five = send(one, near_and_pair(None, 1))
    six = send(choose(two, one), near_and_pair(None, -1))
    seven = send(choose(three, one), near_and_pair(None, 2))
    own = [value, one, two, three, four, five, six, seven]
    swapped = [send(part, sibling) for part in own]
    return own, swapped, grad


def gathered_places(y, z, c):
    y_steps = jnp.where(c == 0, jnp.array([0, 3, 1, 2, 0, 3, 1, 2]), jnp.array([0, 0, 3, 1, 2, 3, 1, 2]))
    z_steps = jnp.where(c == 0, jnp.array([0, 0, 0, 0, 1, 1, 1, 1]), jnp.array([0, 1, 0, 0, 0, 1, 1, 1]))
    return (((z + z_steps) % 2) * 8 + ((y + y_steps) % 4) * 2 + c).astype(jnp.int32)


def place_columns(copy, gathered):
    rows, columns = copy.shape
    width = gathered.shape[1]

    def kernel(copy_ref, gathered_ref, out_ref, semaphore):
        copy = pltpu.make_async_copy(gathered_ref, out_ref.at[:, pl.ds(0, width)], semaphore.at[0])
        copy.start()
        copy.wait()

    hbm = pl.BlockSpec(memory_space=pltpu.HBM)
    return pl.pallas_call(
        kernel,
        in_specs=[hbm, VMEM],
        out_specs=hbm,
        scratch_shapes=[pltpu.SemaphoreType.DMA((1,))],
        out_shape=jax.ShapeDtypeStruct((rows, columns), jnp.bfloat16),
        input_output_aliases={0: 0},
        compiler_params=pltpu.CompilerParams(vmem_limit_bytes=4 * 1024 * 1024),
        name="place_columns",
    )(copy, gathered)


def place_rows(copy, parts, places, rows, columns):
    unit, width = parts[0].shape
    count = len(parts)

    def kernel(places_ref, *refs):
        out_ref, semaphores = refs[-2:]
        copies = []
        for place, ref in enumerate(refs[:count]):
            at = pl.ds(pl.multiple_of(places_ref[place] * unit, unit), unit)
            target = out_ref.at[at, pl.ds(columns - width, width)]
            copies.append(pltpu.make_async_copy(ref, target, semaphores.at[place]))
        for copy in copies:
            copy.start()
        for copy in copies:
            copy.wait()

    hbm = pl.BlockSpec(memory_space=pltpu.HBM)
    old = [] if copy is None else [copy]
    return pl.pallas_call(
        kernel,
        in_specs=[SMEM] + [VMEM] * count + [hbm] * len(old),
        out_specs=hbm,
        scratch_shapes=[pltpu.SemaphoreType.DMA((count,))],
        out_shape=jax.ShapeDtypeStruct((rows, columns), jnp.bfloat16),
        input_output_aliases={1 + count: 0} if old else {},
        compiler_params=pltpu.CompilerParams(vmem_limit_bytes=4 * 1024 * 1024),
        name="place_rows",
    )(places, *parts, *old)


def adamw(grad, master, first_moment, second_moment):
    new_first = 0.9 * first_moment + 0.1 * grad
    new_second = 0.95 * second_moment + 0.05 * (grad * grad)
    first_hat = new_first / (1.0 - 0.9**10)
    second_hat = new_second / (1.0 - 0.95**10)
    step_dir = first_hat / (jnp.sqrt(second_hat) + 1e-08) + 0.1 * master
    new_master = master - 0.02 * step_dir
    return (new_master, new_first, new_second)


def body(layer_input, up_cotangent, master, first_moment, second_moment):
    tokens, columns = layer_input.shape
    total_tokens = tokens * 128
    inter, intra = lax.axis_index("inter"), lax.axis_index("intra")
    c = inter % 2
    x, y, z = intra // 2, (inter // 2) % 4, (intra % 2) * 2 + inter // 8
    where = jnp.stack([jnp.where(c == 0, z, x), jnp.where(c == 0, x, z), y, c]).astype(jnp.int32)
    half = columns // 2

    low, high = layer_input[:, :half], layer_input[:, half:]
    kept = jnp.where(c == 0, low, high)
    given = jnp.where(c == 0, high, low)
    chip_input = jnp.concatenate([kept, send(given, sibling)], axis=0)
    chip_input, swapped = tie(chip_input, up_cotangent)
    other = send(swapped, sibling)

    def spread(value):
        return [send(value, along_rows(step)) for step in (1, 3, 2)]

    starts = [sum(WIDTHS[:place]) for place in range(len(WIDTHS))]
    inputs = [chip_input[:, start : start + width] for start, width in zip(starts, WIDTHS)]
    inputs_0 = [inputs[0], *spread(inputs[0])]
    own, near, last, far = pack(where, up_cotangent, other)
    near, far, inputs_0 = tie(near, far, inputs_0)
    blocks = [own, send(near, along_rows(1)), send(far, along_rows(3)), send(last, along_rows(2))]
    blocks, waiting = tie(blocks, inputs[1])
    inputs_1 = [inputs[1], *spread(waiting)]

    (pieces_0,) = partial_sums(where, blocks, inputs_0, False)
    pieces_0, inputs_1[1:] = tie(pieces_0, inputs_1[1:])
    (part_0,) = lax.psum_scatter(pieces_0, AXES, scatter_dimension=0, axis_index_groups=sum_groups(), tiled=True)
    plus, minus, first, third, keep = partial_sums(where, blocks, inputs_1, True)
    sent_1 = ring_send(plus, minus, along_y)
    turned_1 = ring_turn(first, third, *sent_1, along_y)
    part_0, turned_1 = tie(part_0, turned_1)
    again_0 = direct([part_0[place] for place in range(4)], along_y)
    again_1 = direct([ring_end(keep, *sent_1, *turned_1, place) for place in range(4)], along_sums)
    again_0, again_1 = tie(again_0, again_1)

    rows = jnp.concatenate([summed(again_0), summed(again_1)], axis=1)
    low, high = rows[: rows.shape[0] // 2], rows[rows.shape[0] // 2 :]
    ours = jnp.where(c == 0, low, high)
    theirs = send(jnp.where(c == 0, high, low), sibling)
    scale = 1.0 / math.sqrt(total_tokens)
    grad = wide(jnp.concatenate([jnp.where(c == 0, ours, theirs), jnp.where(c == 0, theirs, ours)], axis=1)) * scale
    fresh = narrow(adamw(grad, master, first_moment, second_moment)[0])

    gathered = lax.all_gather(fresh[:, :SPLIT], "inter", axis=0, tiled=True)
    own_places, other_places = tie(gathered_places(y, z, c), gathered_places(y, z, 1 - c))
    own_parts, other_parts, grad = gather_rows(fresh[:, SPLIT:], c, grad)
    new_copy = place_rows(None, own_parts, own_places, gathered.shape[0], columns)
    new_copy = place_rows(new_copy, other_parts, other_places, gathered.shape[0], columns)
    new_copy = place_columns(new_copy, gathered)
    return (*adamw(grad, master, first_moment, second_moment), new_copy)


def solution(mesh):
    in_specs = (
        P(("inter", "intra"), None),
        P(("inter", "intra"), None),
        P(("intra", "inter"), None),
        P(("intra", "inter"), None),
        P(("intra", "inter"), None),
    )
    out_specs = (
        P(("intra", "inter"), None),
        P(("intra", "inter"), None),
        P(("intra", "inter"), None),
        P("intra", None),
    )
    return jax.shard_map(body, mesh=mesh, in_specs=in_specs, out_specs=out_specs, check_vma=False)
```

```python
import functools
import math

import jax
import jax.numpy as jnp
from jax import lax
from jax.experimental import pallas as pl
from jax.experimental.pallas import tpu as pltpu
from jax.sharding import PartitionSpec as P

AXES = ("inter", "intra")
WIDTHS = (1024, 768)
SPLIT = 2560


def device(x, y, z, c):
    inter = (z % 2) * 8 + y * 2 + c
    intra = x * 2 + z // 2
    return inter * 8 + intra


def permutation(move):
    pairs = []
    for x in range(4):
        for y in range(4):
            for z in range(4):
                for c in range(2):
                    a, b, d, e = move(x, y, z, c)
                    pairs.append((device(x, y, z, c), device(a % 4, b % 4, d % 4, e)))
    return sorted(pairs)


def send(value, move):
    return lax.ppermute(value, AXES, permutation(move))


def sibling(x, y, z, c):
    return x, y, z, 1 - c


def along_rows(step):
    def move(x, y, z, c):
        return (x, y, z + step, c) if c == 0 else (x + step, y, z, c)

    return move


def along_sums(step):
    def move(x, y, z, c):
        return (x + step, y, z, c) if c == 0 else (x, y, z + step, c)

    return move


def along_y(step):
    def move(x, y, z, c):
        return x, y + step, z, c

    return move


def sum_groups():
    groups = [[device(place, y, z, 0) for place in range(4)] for y in range(4) for z in range(4)]
    return groups + [[device(x, y, place, 1) for place in range(4)] for x in range(4) for y in range(4)]


VMEM = pl.BlockSpec(memory_space=pltpu.VMEM)
SMEM = pl.BlockSpec(memory_space=pltpu.SMEM)


def pack(where, mine, other):
    tokens, hidden = mine.shape
    piece = hidden // 16

    def kernel(where_ref, mine_ref, other_ref, *out_refs):
        @pl.loop(0, 4)
        def _(g):
            rows = pl.ds(pl.multiple_of(g * piece, piece), piece)
            for step, out_ref in enumerate(out_refs):
                at = lax.rem(where_ref[0] + step, 4)
                place = jnp.where(where_ref[3] == 0, g * 4 + at, at * 4 + g)
                columns = pl.ds(pl.multiple_of(place * piece, piece), piece)
                both = jnp.concatenate([mine_ref[:, columns], other_ref[:, columns]], axis=0)
                out_ref[rows, :] = both.T

    return pl.pallas_call(
        kernel,
        in_specs=[SMEM, VMEM, VMEM],
        out_specs=[VMEM] * 4,
        out_shape=[jax.ShapeDtypeStruct((hidden // 4, 2 * tokens), mine.dtype)] * 4,
        compiler_params=pltpu.CompilerParams(vmem_limit_bytes=10 * 1024 * 1024),
        cost_estimate=pl.CostEstimate(flops=0, bytes_accessed=8 * tokens * hidden, transcendentals=0),
        name="pack_cotangent",
    )(where, mine, other)


def partial_sums(where, blocks, inputs, ring):
    rows, tokens = blocks[0].shape
    width = inputs[0].shape[1]
    piece = rows // 4
    unit = piece // 8

    def kernel(where_ref, *refs):
        block_refs, input_refs = refs[:4], refs[4:8]
        out_refs = refs[8:-4]
        held, total, turned, semaphores = refs[-4:]

        def loads(g, slot):
            for step, ref in enumerate(block_refs):
                source = ref.at[pl.ds(pl.multiple_of(g * piece, piece), piece), :]
                target = turned.at[slot, :, pl.ds(step * tokens, tokens)]
                yield pltpu.make_async_copy(source, target, semaphores.at[slot, step])

        for load in loads(0, 0):
            load.start()
        for step in range(4):
            held[pl.ds(step * tokens, tokens), :] = input_refs[step][...]

        @pl.loop(0, 4)
        def _(g):
            slot = lax.rem(g, 2)

            @pl.when(g < 3)
            def _():
                for load in loads(g + 1, 1 - slot):
                    load.start()

            for load in loads(g, slot):
                load.wait()
            total[...] = jnp.dot(turned[slot], held[...], preferred_element_type=jnp.float32).astype(jnp.bfloat16)

            step_g = lax.rem(g - where_ref[1] + 4, 4)
            for to_y in range(4):
                step_y = lax.rem(to_y - where_ref[2] + 4, 4)
                if not ring:
                    out_refs[0][g, step_y] = total[pl.ds(to_y * 2 * unit, 2 * unit), :]
                    continue
                plus_ref, minus_ref, first_ref, third_ref, keep_ref = out_refs
                places = [
                    [(keep_ref, 0), (keep_ref, 1)],
                    [(first_ref, None), (plus_ref, 1)],
                    [(plus_ref, 0), (minus_ref, 0)],
                    [(minus_ref, 1), (third_ref, None)],
                ]
                for distance, halves in enumerate(places):

                    @pl.when(step_y == distance)
                    def _(halves=halves, to_y=to_y):
                        for half, (ref, at) in enumerate(halves):
                            value = total[pl.ds((to_y * 2 + half) * unit, unit), :]
                            if at is None:
                                ref[step_g] = value
                            else:
                                ref[at, step_g] = value

    if ring:
        two, one = (2, 4, unit, width), (4, unit, width)
        shapes = (two, two, one, one, two)
    else:
        shapes = ((4, 4, 2 * unit, width),)
    return pl.pallas_call(
        kernel,
        in_specs=[SMEM] + [pl.BlockSpec(memory_space=pltpu.HBM)] * 4 + [VMEM] * 4,
        out_specs=[VMEM] * len(shapes),
        scratch_shapes=[
            pltpu.VMEM((4 * tokens, width), jnp.bfloat16),
            pltpu.VMEM((piece, width), jnp.bfloat16),
            pltpu.VMEM((2, piece, 4 * tokens), jnp.bfloat16),
            pltpu.SemaphoreType.DMA((2, 4)),
        ],
        out_shape=[jax.ShapeDtypeStruct(shape, jnp.bfloat16) for shape in shapes],
        compiler_params=pltpu.CompilerParams(vmem_limit_bytes=16 * 1024 * 1024),
        cost_estimate=pl.CostEstimate(
            flops=2 * 4 * tokens * rows * width,
            bytes_accessed=4 * tokens * (rows + width) * 2 + rows * width * 2,
            transcendentals=0,
        ),
        name="partial_sums",
    )(where, *[pltpu.with_memory_space_constraint(block, pltpu.HBM) for block in blocks], *inputs)


def wide(value):
    return value.astype(jnp.float32)


def narrow(value):
    return value.astype(jnp.bfloat16)


def tie(*values):
    return lax.optimization_barrier(values)


def ring_send(plus, minus, along):
    return send(plus, along(1)), send(minus, along(-1))


def ring_turn(first, third, from_left, from_right, along):
    left = send(narrow(wide(first) + wide(from_left[0])), along(1))
    right = send(narrow(wide(third) + wide(from_right[0])), along(-1))
    return left, right


def ring_end(keep, from_left, from_right, left, right, place):
    low = wide(keep[0, place]) + wide(from_right[1, place]) + wide(left[place])
    high = wide(keep[1, place]) + wide(from_left[1, place]) + wide(right[place])
    return narrow(jnp.concatenate([low, high], axis=0))


def direct(pieces, along):
    return [pieces[0]] + [send(pieces[step], along(step)) for step in (1, 3, 2)]


def summed(received):
    return narrow(sum(wide(value) for value in received))


def near_and_pair(first, second):
    def move(x, y, z, c):
        steps = first if c == 0 else second
        return (x, y, z ^ 1, c) if steps is None else (x, y + steps, z, c)

    return move


def gather_rows(value, c, grad):
    def choose(low, high):
        return jnp.where(c == 0, low, high)

    one = send(value, near_and_pair(1, None))
    two = send(value, near_and_pair(-1, 1))
    three = send(value, near_and_pair(2, -1))
    four = send(value, near_and_pair(None, 2))
    one, grad = tie(one, grad)
    five = send(one, near_and_pair(None, 1))
    six = send(choose(two, one), near_and_pair(None, -1))
    seven = send(choose(three, one), near_and_pair(None, 2))
    own = [value, one, two, three, four, five, six, seven]
    swapped = [send(part, sibling) for part in own]
    return own, swapped, grad


def gathered_places(y, z, c):
    y_steps = jnp.where(c == 0, jnp.array([0, 3, 1, 2, 0, 3, 1, 2]), jnp.array([0, 0, 3, 1, 2, 3, 1, 2]))
    z_steps = jnp.where(c == 0, jnp.array([0, 0, 0, 0, 1, 1, 1, 1]), jnp.array([0, 1, 0, 0, 0, 1, 1, 1]))
    return (((z + z_steps) % 2) * 8 + ((y + y_steps) % 4) * 2 + c).astype(jnp.int32)


def place_columns(copy, gathered):
    rows, columns = copy.shape
    width = gathered.shape[1]

    def kernel(copy_ref, gathered_ref, out_ref, semaphore):
        copy = pltpu.make_async_copy(gathered_ref, out_ref.at[:, pl.ds(0, width)], semaphore.at[0])
        copy.start()
        copy.wait()

    hbm = pl.BlockSpec(memory_space=pltpu.HBM)
    return pl.pallas_call(
        kernel,
        in_specs=[hbm, VMEM],
        out_specs=hbm,
        scratch_shapes=[pltpu.SemaphoreType.DMA((1,))],
        out_shape=jax.ShapeDtypeStruct((rows, columns), jnp.bfloat16),
        input_output_aliases={0: 0},
        compiler_params=pltpu.CompilerParams(vmem_limit_bytes=4 * 1024 * 1024),
        name="place_columns",
    )(copy, gathered)


def place_rows(copy, parts, places, rows, columns):
    unit, width = parts[0].shape
    count = len(parts)

    def kernel(places_ref, *refs):
        out_ref, semaphores = refs[-2:]
        copies = []
        for place, ref in enumerate(refs[:count]):
            at = pl.ds(pl.multiple_of(places_ref[place] * unit, unit), unit)
            target = out_ref.at[at, pl.ds(columns - width, width)]
            copies.append(pltpu.make_async_copy(ref, target, semaphores.at[place]))
        for copy in copies:
            copy.start()
        for copy in copies:
            copy.wait()

    hbm = pl.BlockSpec(memory_space=pltpu.HBM)
    old = [] if copy is None else [copy]
    return pl.pallas_call(
        kernel,
        in_specs=[SMEM] + [VMEM] * count + [hbm] * len(old),
        out_specs=hbm,
        scratch_shapes=[pltpu.SemaphoreType.DMA((count,))],
        out_shape=jax.ShapeDtypeStruct((rows, columns), jnp.bfloat16),
        input_output_aliases={1 + count: 0} if old else {},
        compiler_params=pltpu.CompilerParams(vmem_limit_bytes=4 * 1024 * 1024),
        name="place_rows",
    )(places, *parts, *old)


def adamw(grad, master, first_moment, second_moment):
    new_first = 0.9 * first_moment + 0.1 * grad
    new_second = 0.95 * second_moment + 0.05 * (grad * grad)
    first_hat = new_first / (1.0 - 0.9**10)
    second_hat = new_second / (1.0 - 0.95**10)
    step_dir = first_hat / (jnp.sqrt(second_hat) + 1e-08) + 0.1 * master
    new_master = master - 0.02 * step_dir
    return (new_master, new_first, new_second)


def body(layer_input, up_cotangent, master, first_moment, second_moment):
    tokens, columns = layer_input.shape
    total_tokens = tokens * 128
    inter, intra = lax.axis_index("inter"), lax.axis_index("intra")
    c = inter % 2
    x, y, z = intra // 2, (inter // 2) % 4, (intra % 2) * 2 + inter // 8
    where = jnp.stack([jnp.where(c == 0, z, x), jnp.where(c == 0, x, z), y, c]).astype(jnp.int32)
    half = columns // 2

    low, high = layer_input[:, :half], layer_input[:, half:]
    kept = jnp.where(c == 0, low, high)
    given = jnp.where(c == 0, high, low)
    chip_input = jnp.concatenate([kept, send(given, sibling)], axis=0)
    chip_input, swapped = tie(chip_input, up_cotangent)
    other = send(swapped, sibling)

    def spread(value):
        return [send(value, along_rows(step)) for step in (1, 3, 2)]

    starts = [sum(WIDTHS[:place]) for place in range(len(WIDTHS))]
    inputs = [chip_input[:, start : start + width] for start, width in zip(starts, WIDTHS)]
    inputs_0 = [inputs[0], *spread(inputs[0])]
    own, near, last, far = pack(where, up_cotangent, other)
    near, far, inputs_0 = tie(near, far, inputs_0)
    blocks = [own, send(near, along_rows(1)), send(far, along_rows(3)), send(last, along_rows(2))]
    blocks, waiting = tie(blocks, inputs[1])
    inputs_1 = [inputs[1], *spread(waiting)]

    (pieces_0,) = partial_sums(where, blocks, inputs_0, False)
    pieces_0, inputs_1[1:] = tie(pieces_0, inputs_1[1:])
    (part_0,) = lax.psum_scatter(pieces_0, AXES, scatter_dimension=0, axis_index_groups=sum_groups(), tiled=True)
    plus, minus, first, third, keep = partial_sums(where, blocks, inputs_1, True)
    sent_1 = ring_send(plus, minus, along_y)
    turned_1 = ring_turn(first, third, *sent_1, along_y)
    part_0, turned_1 = tie(part_0, turned_1)
    again_0 = direct([part_0[place] for place in range(4)], along_y)
    again_1 = direct([ring_end(keep, *sent_1, *turned_1, place) for place in range(4)], along_sums)
    again_0, again_1 = tie(again_0, again_1)

    rows = jnp.concatenate([summed(again_0), summed(again_1)], axis=1)
    low, high = rows[: rows.shape[0] // 2], rows[rows.shape[0] // 2 :]
    ours = jnp.where(c == 0, low, high)
    theirs = send(jnp.where(c == 0, high, low), sibling)
    scale = 1.0 / math.sqrt(total_tokens)
    grad = wide(jnp.concatenate([jnp.where(c == 0, ours, theirs), jnp.where(c == 0, theirs, ours)], axis=1)) * scale
    fresh = narrow(adamw(grad, master, first_moment, second_moment)[0])

    gathered = lax.all_gather(fresh[:, :SPLIT], "inter", axis=0, tiled=True)
    own_places, other_places = tie(gathered_places(y, z, c), gathered_places(y, z, 1 - c))
    own_parts, other_parts, grad = gather_rows(fresh[:, SPLIT:], c, grad)
    new_copy = place_rows(None, own_parts, own_places, gathered.shape[0], columns)
    new_copy = place_rows(new_copy, other_parts, other_places, gathered.shape[0], columns)
    new_copy = place_columns(new_copy, gathered)
    return (*adamw(grad, master, first_moment, second_moment), new_copy)


def solution(mesh):
    in_specs = (
        P(("inter", "intra"), None),
        P(("inter", "intra"), None),
        P(("intra", "inter"), None),
        P(("intra", "inter"), None),
        P(("intra", "inter"), None),
    )
    out_specs = (
        P(("intra", "inter"), None),
        P(("intra", "inter"), None),
        P(("intra", "inter"), None),
        P("intra", None),
    )
    return jax.shard_map(body, mesh=mesh, in_specs=in_specs, out_specs=out_specs, check_vma=False)
```

```python
import functools
import math

import jax
import jax.numpy as jnp
from jax import lax
from jax.experimental import pallas as pl
from jax.experimental.pallas import tpu as pltpu
from jax.sharding import PartitionSpec as P

AXES = ("inter", "intra")
WIDTHS = (1024, 768)
SPLIT = 2560


def device(x, y, z, c):
    inter = (z % 2) * 8 + y * 2 + c
    intra = x * 2 + z // 2
    return inter * 8 + intra


def permutation(move):
    pairs = []
    for x in range(4):
        for y in range(4):
            for z in range(4):
                for c in range(2):
                    a, b, d, e = move(x, y, z, c)
                    pairs.append((device(x, y, z, c), device(a % 4, b % 4, d % 4, e)))
    return sorted(pairs)


def send(value, move):
    return lax.ppermute(value, AXES, permutation(move))


def sibling(x, y, z, c):
    return x, y, z, 1 - c


def along_rows(step):
    def move(x, y, z, c):
        return (x, y, z + step, c) if c == 0 else (x + step, y, z, c)

    return move


def along_sums(step):
    def move(x, y, z, c):
        return (x + step, y, z, c) if c == 0 else (x, y, z + step, c)

    return move


def along_y(step):
    def move(x, y, z, c):
        return x, y + step, z, c

    return move


def sum_groups():
    groups = [[device(place, y, z, 0) for place in range(4)] for y in range(4) for z in range(4)]
    return groups + [[device(x, y, place, 1) for place in range(4)] for x in range(4) for y in range(4)]


VMEM = pl.BlockSpec(memory_space=pltpu.VMEM)
SMEM = pl.BlockSpec(memory_space=pltpu.SMEM)


def pack(where, mine, other):
    tokens, hidden = mine.shape
    piece = hidden // 16

    def kernel(where_ref, mine_ref, other_ref, *out_refs):
        @pl.loop(0, 4)
        def _(g):
            rows = pl.ds(pl.multiple_of(g * piece, piece), piece)
            for step, out_ref in enumerate(out_refs):
                at = lax.rem(where_ref[0] + step, 4)
                place = jnp.where(where_ref[3] == 0, g * 4 + at, at * 4 + g)
                columns = pl.ds(pl.multiple_of(place * piece, piece), piece)
                both = jnp.concatenate([mine_ref[:, columns], other_ref[:, columns]], axis=0)
                out_ref[rows, :] = both.T

    return pl.pallas_call(
        kernel,
        in_specs=[SMEM, VMEM, VMEM],
        out_specs=[VMEM] * 4,
        out_shape=[jax.ShapeDtypeStruct((hidden // 4, 2 * tokens), mine.dtype)] * 4,
        compiler_params=pltpu.CompilerParams(vmem_limit_bytes=10 * 1024 * 1024),
        cost_estimate=pl.CostEstimate(flops=0, bytes_accessed=8 * tokens * hidden, transcendentals=0),
        name="pack_cotangent",
    )(where, mine, other)


def partial_sums(where, blocks, inputs, ring):
    rows, tokens = blocks[0].shape
    width = inputs[0].shape[1]
    piece = rows // 4
    unit = piece // 8

    def kernel(where_ref, *refs):
        block_refs, input_refs = refs[:4], refs[4:8]
        out_refs = refs[8:-4]
        held, total, turned, semaphores = refs[-4:]

        def loads(g, slot):
            for step, ref in enumerate(block_refs):
                source = ref.at[pl.ds(pl.multiple_of(g * piece, piece), piece), :]
                target = turned.at[slot, :, pl.ds(step * tokens, tokens)]
                yield pltpu.make_async_copy(source, target, semaphores.at[slot, step])

        for load in loads(0, 0):
            load.start()
        for step in range(4):
            held[pl.ds(step * tokens, tokens), :] = input_refs[step][...]

        @pl.loop(0, 4)
        def _(g):
            slot = lax.rem(g, 2)

            @pl.when(g < 3)
            def _():
                for load in loads(g + 1, 1 - slot):
                    load.start()

            for load in loads(g, slot):
                load.wait()
            total[...] = jnp.dot(turned[slot], held[...], preferred_element_type=jnp.float32).astype(jnp.bfloat16)

            step_g = lax.rem(g - where_ref[1] + 4, 4)
            for to_y in range(4):
                step_y = lax.rem(to_y - where_ref[2] + 4, 4)
                if not ring:
                    out_refs[0][g, step_y] = total[pl.ds(to_y * 2 * unit, 2 * unit), :]
                    continue
                plus_ref, minus_ref, first_ref, third_ref, keep_ref = out_refs
                places = [
                    [(keep_ref, 0), (keep_ref, 1)],
                    [(first_ref, None), (plus_ref, 1)],
                    [(plus_ref, 0), (minus_ref, 0)],
                    [(minus_ref, 1), (third_ref, None)],
                ]
                for distance, halves in enumerate(places):

                    @pl.when(step_y == distance)
                    def _(halves=halves, to_y=to_y):
                        for half, (ref, at) in enumerate(halves):
                            value = total[pl.ds((to_y * 2 + half) * unit, unit), :]
                            if at is None:
                                ref[step_g] = value
                            else:
                                ref[at, step_g] = value

    if ring:
        two, one = (2, 4, unit, width), (4, unit, width)
        shapes = (two, two, one, one, two)
    else:
        shapes = ((4, 4, 2 * unit, width),)
    return pl.pallas_call(
        kernel,
        in_specs=[SMEM] + [pl.BlockSpec(memory_space=pltpu.HBM)] * 4 + [VMEM] * 4,
        out_specs=[VMEM] * len(shapes),
        scratch_shapes=[
            pltpu.VMEM((4 * tokens, width), jnp.bfloat16),
            pltpu.VMEM((piece, width), jnp.bfloat16),
            pltpu.VMEM((2, piece, 4 * tokens), jnp.bfloat16),
            pltpu.SemaphoreType.DMA((2, 4)),
        ],
        out_shape=[jax.ShapeDtypeStruct(shape, jnp.bfloat16) for shape in shapes],
        compiler_params=pltpu.CompilerParams(vmem_limit_bytes=16 * 1024 * 1024),
        cost_estimate=pl.CostEstimate(
            flops=2 * 4 * tokens * rows * width,
            bytes_accessed=4 * tokens * (rows + width) * 2 + rows * width * 2,
            transcendentals=0,
        ),
        name="partial_sums",
    )(where, *[pltpu.with_memory_space_constraint(block, pltpu.HBM) for block in blocks], *inputs)


def wide(value):
    return value.astype(jnp.float32)


def narrow(value):
    return value.astype(jnp.bfloat16)


def tie(*values):
    return lax.optimization_barrier(values)


def ring_send(plus, minus, along):
    return send(plus, along(1)), send(minus, along(-1))


def ring_turn(first, third, from_left, from_right, along):
    left = send(narrow(wide(first) + wide(from_left[0])), along(1))
    right = send(narrow(wide(third) + wide(from_right[0])), along(-1))
    return left, right


def ring_end(keep, from_left, from_right, left, right, place):
    low = wide(keep[0, place]) + wide(from_right[1, place]) + wide(left[place])
    high = wide(keep[1, place]) + wide(from_left[1, place]) + wide(right[place])
    return narrow(jnp.concatenate([low, high], axis=0))


def direct(pieces, along):
    return [pieces[0]] + [send(pieces[step], along(step)) for step in (1, 3, 2)]


def summed(received):
    return narrow(sum(wide(value) for value in received))


def near_and_pair(first, second):
    def move(x, y, z, c):
        steps = first if c == 0 else second
        return (x, y, z ^ 1, c) if steps is None else (x, y + steps, z, c)

    return move


def gather_rows(value, c, grad):
    def choose(low, high):
        return jnp.where(c == 0, low, high)

    one = send(value, near_and_pair(1, None))
    two = send(value, near_and_pair(-1, 1))
    three = send(value, near_and_pair(2, -1))
    four = send(value, near_and_pair(None, 2))
    one, grad = tie(one, grad)
    five = send(one, near_and_pair(None, 1))
    six = send(choose(two, one), near_and_pair(None, -1))
    seven = send(choose(three, one), near_and_pair(None, 2))
    own = [value, one, two, three, four, five, six, seven]
    swapped = [send(part, sibling) for part in own]
    return own, swapped, grad


def gathered_places(y, z, c):
    y_steps = jnp.where(c == 0, jnp.array([0, 3, 1, 2, 0, 3, 1, 2]), jnp.array([0, 0, 3, 1, 2, 3, 1, 2]))
    z_steps = jnp.where(c == 0, jnp.array([0, 0, 0, 0, 1, 1, 1, 1]), jnp.array([0, 1, 0, 0, 0, 1, 1, 1]))
    return (((z + z_steps) % 2) * 8 + ((y + y_steps) % 4) * 2 + c).astype(jnp.int32)


def place_columns(copy, gathered):
    rows, columns = copy.shape
    width = gathered.shape[1]
    count = 8
    chunk = rows // count

    def kernel(copy_ref, gathered_ref, out_ref, held, load_semaphores, store_semaphores):
        loads, stores = [], []
        for k in range(count):
            at = pl.ds(k * chunk, chunk)
            loads.append(pltpu.make_async_copy(gathered_ref.at[at, :], held.at[at, :], load_semaphores.at[k]))
            target = out_ref.at[at, pl.ds(0, width)]
            stores.append(pltpu.make_async_copy(held.at[at, :], target, store_semaphores.at[k]))
        for load in loads:
            load.start()
        for load, store in zip(loads, stores):
            load.wait()
            store.start()
        for store in stores:
            store.wait()

    hbm = pl.BlockSpec(memory_space=pltpu.HBM)
    return pl.pallas_call(
        kernel,
        in_specs=[hbm, hbm],
        out_specs=hbm,
        scratch_shapes=[
            pltpu.VMEM((rows, width), jnp.bfloat16),
            pltpu.SemaphoreType.DMA((count,)),
            pltpu.SemaphoreType.DMA((count,)),
        ],
        out_shape=jax.ShapeDtypeStruct((rows, columns), jnp.bfloat16),
        input_output_aliases={0: 0},
        compiler_params=pltpu.CompilerParams(vmem_limit_bytes=12 * 1024 * 1024),
        name="place_columns",
    )(copy, pltpu.with_memory_space_constraint(gathered, pltpu.HBM))


def place_rows(copy, parts, places, rows, columns):
    unit, width = parts[0].shape
    count = len(parts)

    def kernel(places_ref, *refs):
        out_ref, semaphores = refs[-2:]
        copies = []
        for place, ref in enumerate(refs[:count]):
            at = pl.ds(pl.multiple_of(places_ref[place] * unit, unit), unit)
            target = out_ref.at[at, pl.ds(columns - width, width)]
            copies.append(pltpu.make_async_copy(ref, target, semaphores.at[place]))
        for copy in copies:
            copy.start()
        for copy in copies:
            copy.wait()

    hbm = pl.BlockSpec(memory_space=pltpu.HBM)
    old = [] if copy is None else [copy]
    return pl.pallas_call(
        kernel,
        in_specs=[SMEM] + [VMEM] * count + [hbm] * len(old),
        out_specs=hbm,
        scratch_shapes=[pltpu.SemaphoreType.DMA((count,))],
        out_shape=jax.ShapeDtypeStruct((rows, columns), jnp.bfloat16),
        input_output_aliases={1 + count: 0} if old else {},
        compiler_params=pltpu.CompilerParams(vmem_limit_bytes=4 * 1024 * 1024),
        name="place_rows",
    )(places, *parts, *old)


def adamw(grad, master, first_moment, second_moment):
    new_first = 0.9 * first_moment + 0.1 * grad
    new_second = 0.95 * second_moment + 0.05 * (grad * grad)
    first_hat = new_first / (1.0 - 0.9**10)
    second_hat = new_second / (1.0 - 0.95**10)
    step_dir = first_hat / (jnp.sqrt(second_hat) + 1e-08) + 0.1 * master
    new_master = master - 0.02 * step_dir
    return (new_master, new_first, new_second)


def body(layer_input, up_cotangent, master, first_moment, second_moment):
    tokens, columns = layer_input.shape
    total_tokens = tokens * 128
    inter, intra = lax.axis_index("inter"), lax.axis_index("intra")
    c = inter % 2
    x, y, z = intra // 2, (inter // 2) % 4, (intra % 2) * 2 + inter // 8
    where = jnp.stack([jnp.where(c == 0, z, x), jnp.where(c == 0, x, z), y, c]).astype(jnp.int32)
    half = columns // 2

    low, high = layer_input[:, :half], layer_input[:, half:]
    kept = jnp.where(c == 0, low, high)
    given = jnp.where(c == 0, high, low)
    chip_input = jnp.concatenate([kept, send(given, sibling)], axis=0)
    chip_input, swapped = tie(chip_input, up_cotangent)
    other = send(swapped, sibling)

    def spread(value):
        return [send(value, along_rows(step)) for step in (1, 3, 2)]

    starts = [sum(WIDTHS[:place]) for place in range(len(WIDTHS))]
    inputs = [chip_input[:, start : start + width] for start, width in zip(starts, WIDTHS)]
    inputs_0 = [inputs[0], *spread(inputs[0])]
    own, near, last, far = pack(where, up_cotangent, other)
    near, far, inputs_0 = tie(near, far, inputs_0)
    blocks = [own, send(near, along_rows(1)), send(far, along_rows(3)), send(last, along_rows(2))]
    blocks, waiting = tie(blocks, inputs[1])
    inputs_1 = [inputs[1], *spread(waiting)]

    (pieces_0,) = partial_sums(where, blocks, inputs_0, False)
    pieces_0, inputs_1[1:] = tie(pieces_0, inputs_1[1:])
    (part_0,) = lax.psum_scatter(pieces_0, AXES, scatter_dimension=0, axis_index_groups=sum_groups(), tiled=True)
    plus, minus, first, third, keep = partial_sums(where, blocks, inputs_1, True)
    sent_1 = ring_send(plus, minus, along_y)
    turned_1 = ring_turn(first, third, *sent_1, along_y)
    part_0, turned_1 = tie(part_0, turned_1)
    again_0 = direct([part_0[place] for place in range(4)], along_y)
    again_1 = direct([ring_end(keep, *sent_1, *turned_1, place) for place in range(4)], along_sums)
    again_0, again_1 = tie(again_0, again_1)

    rows = jnp.concatenate([summed(again_0), summed(again_1)], axis=1)
    low, high = rows[: rows.shape[0] // 2], rows[rows.shape[0] // 2 :]
    ours = jnp.where(c == 0, low, high)
    theirs = send(jnp.where(c == 0, high, low), sibling)
    scale = 1.0 / math.sqrt(total_tokens)
    grad = wide(jnp.concatenate([jnp.where(c == 0, ours, theirs), jnp.where(c == 0, theirs, ours)], axis=1)) * scale
    fresh = narrow(adamw(grad, master, first_moment, second_moment)[0])

    gathered = lax.all_gather(fresh[:, :SPLIT], "inter", axis=0, tiled=True)
    own_places, other_places = tie(gathered_places(y, z, c), gathered_places(y, z, 1 - c))
    own_parts, other_parts, grad = gather_rows(fresh[:, SPLIT:], c, grad)
    new_copy = place_rows(None, own_parts, own_places, gathered.shape[0], columns)
    new_copy = place_rows(new_copy, other_parts, other_places, gathered.shape[0], columns)
    new_copy = place_columns(new_copy, gathered)
    return (*adamw(grad, master, first_moment, second_moment), new_copy)


def solution(mesh):
    in_specs = (
        P(("inter", "intra"), None),
        P(("inter", "intra"), None),
        P(("intra", "inter"), None),
        P(("intra", "inter"), None),
        P(("intra", "inter"), None),
    )
    out_specs = (
        P(("intra", "inter"), None),
        P(("intra", "inter"), None),
        P(("intra", "inter"), None),
        P("intra", None),
    )
    return jax.shard_map(body, mesh=mesh, in_specs=in_specs, out_specs=out_specs, check_vma=False)
```
